256 devices in a mesh: blk: 32 (over y, x, core), grp: 8 (over z).
Axes of the slice: x: 4, y: 4, z: 8, core: 2. Of those that a mesh axis runs over, the one named last changes fastest.
Arguments:
- rhs: float32 [7, 262144], P(None, ('blk', 'grp')), may hold values from -36 to 36
- diag_blocks: float32 [7, 7, 262144], P(None, None, ('blk', 'grp'))
- lower_blocks: float32 [7, 7, 262144], P(None, None, ('blk', 'grp')), may hold values from -1.5 to 1.5
- upper_blocks: float32 [7, 7, 262144], P(None, None, ('blk', 'grp')), may hold values from -1.5 to 1.5
- precond: float32 [7, 7, 262144], P(None, None, ('blk', 'grp'))
- coupling: float32 [256, 7, 7, 32, 128], P(('blk', 'grp')), may hold values from -1.5 to 1.5
- send_cells: int32 [256, 32, 128], P(('blk', 'grp')), may hold values from 0 to 1023
- recv_cells: int32 [256, 32, 128], P(('blk', 'grp')), may hold values from 0 to 1023
- halo_len: int32 [256, 32], P(('blk', 'grp')), may hold values from 0 to 128, as said below
Outputs:
- adjoint: float32 [7, 262144], P(None, ('blk', 'grp'))
- residual: float32 [7, 262144], P(None, ('blk', 'grp'))
The draws below stay inside these ranges and needn't reach their ends.
Inputs may be any that keep to these rules, and one draw needn't show every extreme that they name: `halo_len`: every device has at least one peer with exactly 128 face cells.
All inputs are finite; a program needn't handle non-finite values.
Results may differ from the reference program's by a relative error of at most 0.0013.
Values sent between devices are 32-bit elements; how exact they have to be, the bound alone decides.
No kernel may reach another device: no remote copies, remote signals or barrier semaphores. Data moves between devices by JAX's collectives and lax.ppermute only.
A program may use at most 128 MiB of HBM per device.

```python
import jax
import jax.numpy as jnp
from jax import lax

FIELDS = 7
NC = 1024
HALO = 128
ITERS = 4
CELLS = 262144
N_BLK = 32
N_GRP = 8
DEVICES = 256


def dominant(key, diag_lo, diag_hi, off_scale):
    key_off, key_diag = jax.random.split(key)
    off = jax.random.normal(key_off, (FIELDS, FIELDS, CELLS), jnp.float32) * off_scale
    diag = jnp.exp(jax.random.uniform(key_diag, (FIELDS, CELLS), jnp.float32, jnp.log(diag_lo), jnp.log(diag_hi)))
    unit = jnp.eye(FIELDS, dtype=jnp.float32)[:, :, None]
    return off * (1.0 - unit) + unit * diag[:, None, :]


def draw_diag_blocks(key, part):
    key = jax.random.fold_in(key, 1)
    return dominant(key, 6.0, 13.0, 0.4)


def draw_precond(key, part):
    key = jax.random.fold_in(key, 2)
    return dominant(key, 0.08, 0.2, 0.025)


def draw_halo_len(key, part):
    key = jax.random.fold_in(key, 3)
    key_count, key_pick, key_len = jax.random.split(key, 3)
    partners = jax.random.randint(key_count, (DEVICES, 1), N_BLK * 3 // 16, N_BLK * 7 // 16 + 1)
    picked = jax.random.randint(key_pick, (DEVICES, N_BLK), 0, N_BLK) < partners
    lengths = jax.random.randint(key_len, (DEVICES, N_BLK), HALO // 2, HALO + 1) * picked.astype(jnp.int32)
    device_ids = jnp.arange(DEVICES, dtype=jnp.int32)[:, None]
    peer_ids = jnp.arange(N_BLK, dtype=jnp.int32)[None, :]
    full = peer_ids == (device_ids // N_GRP + 1) % N_BLK
    return jnp.where(full, HALO, lengths).astype(jnp.int32)


def touch_ends(entries, key, least, top_value):
    extent = entries.shape
    index_at = [jax.random.randint(jax.random.fold_in(key, axis), (), 0, extent[axis]) for axis in range(len(extent))]
    entries = entries.at[tuple(index_at)].set(least)
    longest = extent.index(max(extent))
    index_at[longest] = (index_at[longest] + 1) % extent[longest]
    return entries.at[tuple(index_at)].set(top_value)


def levels(rng, dims, shards, low, largest):
    level, own = 1.0, jax.random.fold_in(rng, 6)
    for position, blocks in shards:
        heights = jnp.exp(jax.random.uniform(jax.random.fold_in(own, position), (blocks,), jnp.float32, low / len(shards), largest / len(shards)))
        level = level * jnp.repeat(heights, dims[position] // blocks).reshape([-1 if axis == position else 1 for axis in range(len(dims))])
    return level


def scatter_about(rng, dims, scale, most, pieces=(), kind=jnp.bfloat16):
    values = jax.random.normal(rng, dims, jnp.float32) * scale
    if len(pieces) > 0:
        values = levels(rng, dims, pieces, -0.22, 0.18) * values
    return jnp.clip(values, min=-most, max=most).astype(kind)


def setup_inputs(seed: int = 0) -> dict:
    splits = jax.random.split(jax.random.key(seed), 10)
    rhs = scatter_about(splits[0], (FIELDS, CELLS), 6.0, 36.0, ((1, 256),), jnp.float32)
    diag_blocks = draw_diag_blocks(jax.random.fold_in(splits[9], 71), 0)
    lower_blocks = scatter_about(splits[2], (FIELDS, FIELDS, CELLS), 0.25, 1.5, ((2, 256),), jnp.float32)
    upper_blocks = scatter_about(splits[3], (FIELDS, FIELDS, CELLS), 0.25, 1.5, ((2, 256),), jnp.float32)
    precond = draw_precond(jax.random.fold_in(splits[9], 71), 0)
    coupling = scatter_about(splits[5], (DEVICES, FIELDS, FIELDS, N_BLK, HALO), 0.25, 1.5, ((0, 256),), jnp.float32)
    send_cells = touch_ends(jax.random.randint(splits[6], (DEVICES, N_BLK, HALO), 0, NC), jax.random.fold_in(splits[6], 1), 0, NC - 1).astype(jnp.int32)
    recv_cells = touch_ends(jax.random.randint(splits[7], (DEVICES, N_BLK, HALO), 0, NC), jax.random.fold_in(splits[7], 1), 0, NC - 1).astype(jnp.int32)
    halo_len = draw_halo_len(jax.random.fold_in(splits[9], 71), 0)
    return {"rhs": rhs, "diag_blocks": diag_blocks, "lower_blocks": lower_blocks, "upper_blocks": upper_blocks, "precond": precond, "coupling": coupling, "send_cells": send_cells, "recv_cells": recv_cells, "halo_len": halo_len}


def mixing(blocks, field):
    total = blocks[:, 0] * field[0][None]
    for inner in range(1, field.shape[0]):
        total = total + blocks[:, inner] * field[inner][None]
    return total

def operate(field, diag_blocks, lower_blocks, upper_blocks, masked, send_cells, recv_cells):
    cube = field.reshape(FIELDS, DEVICES, NC)
    zero_col = jnp.zeros((FIELDS, DEVICES, 1), jnp.float32)
    before = jnp.concatenate([zero_col, cube[:, :, :-1]], axis=2).reshape(FIELDS, CELLS)
    after = jnp.concatenate([cube[:, :, 1:], zero_col], axis=2).reshape(FIELDS, CELLS)
    local = mixing(diag_blocks, field) + mixing(lower_blocks, before) + mixing(upper_blocks, after)
    outgoing = jax.vmap(lambda piece, cells: piece[:, cells], in_axes=(1, 0), out_axes=0)(cube, send_cells)
    term = jax.vmap(mixing, in_axes=(0, 0), out_axes=0)(masked, outgoing)
    term = term.reshape(N_BLK, N_GRP, FIELDS, N_BLK, HALO).transpose(3, 1, 2, 0, 4).reshape(DEVICES, FIELDS, N_BLK, HALO)
    local_cube = local.reshape(FIELDS, DEVICES, NC)

    def add_faces(piece, cells, values):
        return piece.at[:, cells.reshape(-1)].add(values.reshape(FIELDS, -1))
    local_cube = jax.vmap(add_faces, in_axes=(1, 0, 0), out_axes=1)(local_cube, recv_cells, term)
    return local_cube.reshape(FIELDS, CELLS)

def reference(rhs, diag_blocks, lower_blocks, upper_blocks, precond, coupling, send_cells, recv_cells, halo_len):
    slots = jnp.arange(HALO, dtype=jnp.int32)
    live = (slots[None, None, :] < halo_len[:, :, None]).astype(jnp.float32)
    masked = coupling * live[:, None, None, :, :]

    def apply_op(field):
        return operate(field, diag_blocks, lower_blocks, upper_blocks, masked, send_cells, recv_cells)
    beta = jnp.sqrt(jnp.sum(rhs * rhs))
    basis = [rhs / beta]
    hess = jnp.zeros((ITERS + 1, ITERS), jnp.float32)
    for col in range(ITERS):
        product = apply_op(mixing(precond, basis[col]))
        proj = jnp.stack([jnp.sum(vector * product) for vector in basis])
        remain = product
        for index in range(col + 1):
            remain = remain - proj[index] * basis[index]
        height = jnp.sqrt(jnp.sum(remain * remain))
        hess = hess.at[:col + 1, col].set(proj).at[col + 1, col].set(height)
        basis.append(remain / height)
    gram = jnp.dot(hess.T, hess, precision=lax.Precision.HIGHEST)
    factor = jnp.linalg.cholesky(gram)
    coef = jax.scipy.linalg.cho_solve((factor, True), beta * hess[0])
    combo = coef[0] * basis[0]
    for index in range(1, ITERS):
        combo = combo + coef[index] * basis[index]
    adjoint = mixing(precond, combo)
    residual = rhs - apply_op(adjoint)
    return (adjoint, residual)
```

```python
import functools

import jax
import jax.numpy as jnp
from jax import lax
from jax.experimental import pallas as pl
from jax.experimental.pallas import tpu as pltpu
from jax.sharding import PartitionSpec as P

ITERS = 4
F = 7
LANES = 128
BOTH = ("blk", "grp")


def mixing(blocks, field):
    total = blocks[:, 0] * field[0][None]
    for inner in range(1, field.shape[0]):
        total = total + blocks[:, inner] * field[inner][None]
    return total


def operate(field, diag_blocks, lower_blocks, upper_blocks, masked, send_flat, recv_flat):
    fields = field.shape[0]
    peers, width = masked.shape[2:]
    zero_col = jnp.zeros((fields, 1), jnp.float32)
    before = jnp.concatenate([zero_col, field[:, :-1]], axis=1)
    after = jnp.concatenate([field[:, 1:], zero_col], axis=1)
    outgoing = jnp.take(field, send_flat, axis=1).reshape(fields, peers, width)
    term = lax.all_to_all(mixing(masked, outgoing), "blk", split_axis=1, concat_axis=1, tiled=True)
    local = mixing(diag_blocks, field) + mixing(lower_blocks, before) + mixing(upper_blocks, after)
    return local.at[:, recv_flat].add(term.reshape(fields, -1))


def arnoldi(rhs, diag_blocks, lower_blocks, upper_blocks, precond, coupling, send_cells, recv_cells, halo_len):
    slots = jnp.arange(coupling.shape[4], dtype=jnp.int32)
    live = (slots[None, :] < halo_len[0][:, None]).astype(jnp.float32)
    masked = coupling[0] * live[None, None, :, :]
    send_flat = send_cells[0].reshape(-1)
    recv_flat = recv_cells[0].reshape(-1)

    def apply_op(field):
        return operate(field, diag_blocks, lower_blocks, upper_blocks, masked, send_flat, recv_flat)

    beta = jnp.sqrt(lax.psum(jnp.sum(rhs * rhs), BOTH))
    basis = [rhs / beta]
    hess = jnp.zeros((ITERS + 1, ITERS), jnp.float32)
    for col in range(ITERS):
        product = apply_op(mixing(precond, basis[col]))
        proj = lax.psum(jnp.stack([jnp.sum(vector * product) for vector in basis]), BOTH)
        remain = product
        for index in range(col + 1):
            remain = remain - proj[index] * basis[index]
        height = jnp.sqrt(lax.psum(jnp.sum(remain * remain), BOTH))
        hess = hess.at[: col + 1, col].set(proj).at[col + 1, col].set(height)
        basis.append(remain / height)
    gram = jnp.dot(hess.T, hess, precision=lax.Precision.HIGHEST)
    factor = jnp.linalg.cholesky(gram)
    coef = jax.scipy.linalg.cho_solve((factor, True), beta * hess[0])
    combo = coef[0] * basis[0]
    for index in range(1, ITERS):
        combo = combo + coef[index] * basis[index]
    adjoint = mixing(precond, combo)
    return adjoint, rhs - apply_op(adjoint)


def two_sum(a, b):
    s = a + b
    t = s - a
    return s, (a - (s - t)) + (b - t)


def quick_sum(a, b):
    s = a + b
    return s, b - (s - a)


def halves(a):
    t = a * 4097.0
    high = t - (t - a)
    return high, a - high


def two_prod(a, ah, al, b, bh, bl):
    p = a * b
    return p, ((ah * bh - p) + ah * bl + al * bh) + al * bl


def dd_add(a, b):
    s, e = two_sum(a[0], b[0])
    return quick_sum(s, e + (a[1] + b[1]))


def dd_mul(a, b):
    p, e = two_prod(a[0], *halves(a[0]), b[0], *halves(b[0]))
    return quick_sum(p, e + (a[0] * b[1] + a[1] * b[0]))


def dd_neg(a):
    return -a[0], -a[1]


def dd_div(a, b):
    q = a[0] / b[0]
    rest = dd_add(a, dd_neg(dd_mul(b, (q, jnp.zeros_like(q)))))
    return quick_sum(q, rest[0] / b[0])


def row_sums(parts):
    rows = [jnp.sum(part, axis=0, keepdims=True) for part in parts]
    return jnp.concatenate(rows + [jnp.zeros_like(rows[0])], axis=0)


def precondition(pre_ref, u):
    return row_sums([pre_ref[i] * u[:F] for i in range(F)])


def write_message(z, coup_ref, send_ref, halo_ref, msg_ref):
    cells = z.shape[1]
    tiles = cells // LANES
    peers = send_ref.shape[1]
    source = [
        [jnp.broadcast_to(z[f : f + 1, t * LANES : (t + 1) * LANES], (8, LANES)) for t in range(tiles)]
        for f in range(F)
    ]
    lanes = lax.broadcasted_iota(jnp.int32, (8, LANES), 1)
    rows = lax.broadcasted_iota(jnp.int32, (8, peers), 0)
    cols = lax.broadcasted_iota(jnp.int32, (8, peers), 1)
    lens = jnp.broadcast_to(halo_ref[...], (8, peers))
    for q in range(peers // 8):
        cell = send_ref[0, q * 8 : (q + 1) * 8, :]
        low = cell & (LANES - 1)
        high = cell >> 7
        size = jnp.sum(jnp.where(cols == rows + q * 8, lens, 0), axis=1, keepdims=True)
        live = lanes < size
        taken = []
        for f in range(F):
            got = jnp.take_along_axis(source[f][0], low, axis=1, mode="promise_in_bounds")
            for t in range(1, tiles):
                other = jnp.take_along_axis(source[f][t], low, axis=1, mode="promise_in_bounds")
                got = jnp.where(high == t, other, got)
            taken.append(got)
        for i in range(F):
            total = coup_ref[0, i, 0, q * 8 : (q + 1) * 8, :] * taken[0]
            for j in range(1, F):
                total = total + coup_ref[0, i, j, q * 8 : (q + 1) * 8, :] * taken[j]
            msg_ref[pl.ds(q * 64 + i, 8, stride=8), :] = jnp.where(live, total, 0.0)
        msg_ref[pl.ds(q * 64 + F, 8, stride=8), :] = jnp.zeros((8, LANES), jnp.float32)


def scatter(recv_ref, cells_ref, tiles):
    peers = cells_ref.shape[1]
    spots = lax.broadcasted_iota(jnp.int32, (LANES, LANES), 0)
    left, right = [], []
    for s in range(peers):
        x = recv_ref[s * 8 : (s + 1) * 8, :]
        first = x.astype(jnp.bfloat16).astype(jnp.float32)
        rest = x - first
        second = rest.astype(jnp.bfloat16).astype(jnp.float32)
        third = rest - second
        cell = cells_ref[0, s : s + 1, :]
        low = jnp.broadcast_to(cell & (LANES - 1), (LANES, LANES))
        high = jnp.broadcast_to(cell >> 7, (8, LANES))
        pieces = []
        for t in range(tiles):
            here = high == t
            pieces += [jnp.where(here, part, 0.0) for part in (first, second, third)]
        left.append(jnp.concatenate(pieces, axis=0).astype(jnp.bfloat16))
        right.append(jnp.where(spots == low, 1.0, 0.0).astype(jnp.bfloat16))
    total = lax.dot_general(
        jnp.concatenate(left, axis=1),
        jnp.concatenate(right, axis=1),
        (((1,), (1,)), ((), ())),
        preferred_element_type=jnp.float32,
    )
    out = []
    for t in range(tiles):
        a, b, c = (total[t * 24 + 8 * k : t * 24 + 8 * k + 8] for k in range(3))
        out.append((c + b) + a)
    return jnp.concatenate(out, axis=1)


def products(us, last):
    cells = last.shape[1]
    tiles = [slice(t * LANES, (t + 1) * LANES) for t in range(cells // LANES)]
    lh, ll = halves(last)
    rows = lax.broadcasted_iota(jnp.int32, (8, LANES), 0)
    hi = jnp.zeros((8, LANES), jnp.float32)
    lo = jnp.zeros((8, LANES), jnp.float32)
    for i, u in enumerate(us):
        uh, ul = halves(u)
        terms = []
        for t in tiles:
            terms.append(two_prod(u[:, t], uh[:, t], ul[:, t], last[:, t], lh[:, t], ll[:, t]))
        while len(terms) > 1:
            terms = [dd_add(terms[k], terms[k + 1]) for k in range(0, len(terms), 2)]
        total = terms[0]
        for shift in (4, 2, 1):
            total = dd_add(total, tuple(pltpu.roll(v, shift, 0) for v in total))
        hi = jnp.where(rows == i, total[0], hi)
        lo = jnp.where(rows == i, total[1], lo)
    total = (hi, lo)
    for shift in (64, 32, 16, 8, 4, 2, 1):
        total = dd_add(total, tuple(pltpu.roll(v, shift, 1) for v in total))
    return total


def first_kernel(rhs_ref, pre_ref, coup_ref, send_ref, halo_ref, u_ref, z_ref, msg_ref):
    u = jnp.concatenate([rhs_ref[...], jnp.zeros((1, rhs_ref.shape[1]), jnp.float32)], axis=0)
    z = precondition(pre_ref, u)
    u_ref[...] = u
    z_ref[...] = z
    write_message(z, coup_ref, send_ref, halo_ref, msg_ref)


def local_kernel(count, z_ref, diag_ref, low_ref, up_ref, *refs):
    u_refs, (y_ref, gram_ref) = refs[:count], refs[count:]
    z = z_ref[...]
    cells = z.shape[1]
    col = lax.broadcasted_iota(jnp.int32, z.shape, 1)
    before = jnp.where(col == 0, 0.0, pltpu.roll(z, 1, 1))[:F]
    after = jnp.where(col == cells - 1, 0.0, pltpu.roll(z, cells - 1, 1))[:F]
    z = z[:F]
    y_ref[...] = row_sums([diag_ref[i] * z + low_ref[i] * before + up_ref[i] * after for i in range(F)])
    us = [ref[...] for ref in u_refs]
    gram_ref[0], gram_ref[1] = products(us, us[-1])


def step_kernel(recv_ref, cells_ref, y_ref, pre_ref, coup_ref, send_ref, halo_ref, u_ref, z_ref, msg_ref):
    u = y_ref[...] + scatter(recv_ref, cells_ref, y_ref.shape[1] // LANES)
    z = precondition(pre_ref, u)
    u_ref[...] = u
    z_ref[...] = z
    write_message(z, coup_ref, send_ref, halo_ref, msg_ref)


def last_kernel(recv_ref, cells_ref, y_ref, *refs):
    u_refs, gram_refs, (u_ref, msg_ref) = refs[:ITERS], refs[ITERS : 2 * ITERS], refs[2 * ITERS :]
    u = y_ref[...] + scatter(recv_ref, cells_ref, y_ref.shape[1] // LANES)
    u_ref[...] = u
    columns = [(ref[0], ref[1]) for ref in gram_refs]
    columns.append(products([ref[...] for ref in u_refs] + [u], u))
    lane = lax.broadcasted_iota(jnp.int32, (1, LANES), 1)
    row = jnp.zeros((1, LANES), jnp.float32)
    for j in range(ITERS + 1):
        for i in range(j + 1):
            for part in range(2):
                row = jnp.where(lane == part * 64 + 8 * j + i, columns[j][part][i : i + 1], row)
    msg_ref[...] = jnp.broadcast_to(row, msg_ref.shape)


def finish_kernel(count, got_ref, *refs):
    u_refs, z_refs = refs[: ITERS + 1], refs[ITERS + 1 : 2 * ITERS + 1]
    adj_ref, res_ref, flag_ref = refs[2 * ITERS + 1 :]
    lane = lax.broadcasted_iota(jnp.int32, (8, LANES), 1)
    rows = [got_ref[8 * k : 8 * k + 8, :] for k in range(count // 8)]
    pairs = [(jnp.where(lane < 64, row, 0.0), pltpu.roll(jnp.where(lane < 64, 0.0, row), 64, 1)) for row in rows]
    while len(pairs) > 1:
        pairs = [dd_add(pairs[k], pairs[k + 1]) for k in range(0, len(pairs), 2)]
    total = pairs[0]
    for shift in (4, 2, 1):
        total = dd_add(total, tuple(pltpu.roll(v, shift, 0) for v in total))

    def entry(i, j):
        i, j = min(i, j), max(i, j)
        at = 8 * j + i
        return tuple(jnp.broadcast_to(v[0:1, at : at + 1], (1, LANES)) for v in total)

    n = ITERS
    mat = [[entry(i + 1, j + 1) if j >= i else None for j in range(n)] for i in range(n)]
    vec = [entry(0, i + 1) for i in range(n)]
    norms = [mat[i][i][0] for i in range(n)]
    first = entry(0, 0)
    ok = (first[0] > 1e-20) & (first[0] < 1e30)
    left = first
    scaled = [None] * n
    factor = [[None] * n for _ in range(n)]
    for k in range(n):
        pivot = mat[k][k]
        ok = ok & (norms[k] > 1e-20) & (norms[k] < 1e30) & (pivot[0] > 1e-9 * norms[k])
        scaled[k] = dd_div(vec[k], pivot)
        left = dd_add(left, dd_neg(dd_mul(vec[k], scaled[k])))
        for j in range(k + 1, n):
            factor[k][j] = dd_div(mat[k][j], pivot)
        for i in range(k + 1, n):
            for j in range(i, n):
                mat[i][j] = dd_add(mat[i][j], dd_neg(dd_mul(factor[k][i], mat[k][j])))
            vec[i] = dd_add(vec[i], dd_neg(dd_mul(factor[k][i], vec[k])))
    coef = [None] * n
    for k in reversed(range(n)):
        value = scaled[k]
        for j in range(k + 1, n):
            value = dd_add(value, dd_neg(dd_mul(factor[k][j], coef[j])))
        coef[k] = value
    reach = jnp.zeros((1, LANES), jnp.float32)
    for k in range(n):
        reach = reach + jnp.abs(coef[k][0]) * jnp.sqrt(norms[k])
    ok = ok & (reach * reach < 1e7 * left[0])
    flag_ref[0] = jnp.min(jnp.where(ok, 1, 0))
    cells = adj_ref.shape[1]
    weight = [jnp.broadcast_to(coef[k][0][:, :1], (8, cells)) for k in range(n)]
    adj = weight[0] * z_refs[0][...]
    res = u_refs[0][...] - weight[0] * u_refs[1][...]
    for k in range(1, n):
        adj = adj + weight[k] * z_refs[k][...]
        res = res - weight[k] * u_refs[k + 1][...]
    adj_ref[...] = adj[:F]
    res_ref[...] = res[:F]


def shape(*dims):
    return jax.ShapeDtypeStruct(dims, jnp.float32)


def call(kernel, out, *args, name):
    return pl.pallas_call(
        kernel,
        out_shape=out,
        name=name,
        in_specs=[pl.BlockSpec(memory_space=pltpu.VMEM)] * len(args),
        out_specs=jax.tree.map(
            lambda o: pl.BlockSpec(memory_space=pltpu.SMEM if o.dtype == jnp.int32 else pltpu.VMEM), out
        ),
        compiler_params=pltpu.CompilerParams(vmem_limit_bytes=24 * 2**20),
    )(*args)


def per_device(rhs, diag_blocks, lower_blocks, upper_blocks, precond, coupling, send_cells, recv_cells, halo_len):
    fields, cells = rhs.shape
    peers = send_cells.shape[1]
    count = peers * lax.axis_size("grp")
    face = (precond, coupling, send_cells, halo_len)
    vector = shape(8, cells)
    message = shape(peers * 8, LANES)
    u, z, msg = call(first_kernel, (vector, vector, message), rhs, *face, name="first")
    us, zs, grams = [u], [z], []
    for col in range(ITERS):
        got = lax.all_to_all(msg.reshape(peers, 8, LANES), "blk", 0, 0, tiled=True)
        y, gram = call(
            functools.partial(local_kernel, col + 1),
            (vector, shape(2, 8, LANES)),
            zs[col], diag_blocks, lower_blocks, upper_blocks, *us,
            name="local",
        )
        grams.append(gram)
        got = got.reshape(peers * 8, LANES)
        if col < ITERS - 1:
            u, z, msg = call(step_kernel, (vector, vector, message), got, recv_cells, y, *face, name="step")
            zs.append(z)
        else:
            u, msg = call(last_kernel, (vector, shape(count, LANES)), got, recv_cells, y, *us, *grams, name="last")
        us.append(u)
    got = lax.all_to_all(msg, BOTH, 0, 0, tiled=True)
    adjoint, residual, flag = call(
        functools.partial(finish_kernel, count),
        (shape(fields, cells), shape(fields, cells), jax.ShapeDtypeStruct((1,), jnp.int32)),
        got, *us, *zs,
        name="finish",
    )
    return lax.cond(
        flag[0] == 1,
        lambda *args: (adjoint, residual),
        arnoldi,
        rhs, diag_blocks, lower_blocks, upper_blocks, precond, coupling, send_cells, recv_cells, halo_len,
    )


def solution(mesh):
    return jax.shard_map(
        per_device,
        mesh=mesh,
        in_specs=(
            P(None, BOTH),
            P(None, None, BOTH),
            P(None, None, BOTH),
            P(None, None, BOTH),
            P(None, None, BOTH),
            P(BOTH, None, None, None, None),
            P(BOTH, None, None),
            P(BOTH, None, None),
            P(BOTH, None),
        ),
        out_specs=(P(None, BOTH), P(None, BOTH)),
        check_vma=False,
    )
```

```python
import functools

import jax
import jax.numpy as jnp
from jax import lax
from jax.experimental import pallas as pl
from jax.experimental.pallas import tpu as pltpu
from jax.sharding import PartitionSpec as P

ITERS = 4
F = 7
LANES = 128
BOTH = ("blk", "grp")


def mixing(blocks, field):
    total = blocks[:, 0] * field[0][None]
    for inner in range(1, field.shape[0]):
        total = total + blocks[:, inner] * field[inner][None]
    return total


def operate(field, diag_blocks, lower_blocks, upper_blocks, masked, send_flat, recv_flat):
    fields = field.shape[0]
    peers, width = masked.shape[2:]
    zero_col = jnp.zeros((fields, 1), jnp.float32)
    before = jnp.concatenate([zero_col, field[:, :-1]], axis=1)
    after = jnp.concatenate([field[:, 1:], zero_col], axis=1)
    outgoing = jnp.take(field, send_flat, axis=1).reshape(fields, peers, width)
    term = lax.all_to_all(mixing(masked, outgoing), "blk", split_axis=1, concat_axis=1, tiled=True)
    local = mixing(diag_blocks, field) + mixing(lower_blocks, before) + mixing(upper_blocks, after)
    return local.at[:, recv_flat].add(term.reshape(fields, -1))


def arnoldi(rhs, diag_blocks, lower_blocks, upper_blocks, precond, coupling, send_cells, recv_cells, halo_len):
    slots = jnp.arange(coupling.shape[4], dtype=jnp.int32)
    live = (slots[None, :] < halo_len[0][:, None]).astype(jnp.float32)
    masked = coupling[0] * live[None, None, :, :]
    send_flat = send_cells[0].reshape(-1)
    recv_flat = recv_cells[0].reshape(-1)

    def apply_op(field):
        return operate(field, diag_blocks, lower_blocks, upper_blocks, masked, send_flat, recv_flat)

    beta = jnp.sqrt(lax.psum(jnp.sum(rhs * rhs), BOTH))
    basis = [rhs / beta]
    hess = jnp.zeros((ITERS + 1, ITERS), jnp.float32)
    for col in range(ITERS):
        product = apply_op(mixing(precond, basis[col]))
        proj = lax.psum(jnp.stack([jnp.sum(vector * product) for vector in basis]), BOTH)
        remain = product
        for index in range(col + 1):
            remain = remain - proj[index] * basis[index]
        height = jnp.sqrt(lax.psum(jnp.sum(remain * remain), BOTH))
        hess = hess.at[: col + 1, col].set(proj).at[col + 1, col].set(height)
        basis.append(remain / height)
    gram = jnp.dot(hess.T, hess, precision=lax.Precision.HIGHEST)
    factor = jnp.linalg.cholesky(gram)
    coef = jax.scipy.linalg.cho_solve((factor, True), beta * hess[0])
    combo = coef[0] * basis[0]
    for index in range(1, ITERS):
        combo = combo + coef[index] * basis[index]
    adjoint = mixing(precond, combo)
    return adjoint, rhs - apply_op(adjoint)


def two_sum(a, b):
    s = a + b
    t = s - a
    return s, (a - (s - t)) + (b - t)


def quick_sum(a, b):
    s = a + b
    return s, b - (s - a)


def halves(a):
    t = a * 4097.0
    high = t - (t - a)
    return high, a - high


def two_prod(a, ah, al, b, bh, bl):
    p = a * b
    return p, ((ah * bh - p) + ah * bl + al * bh) + al * bl


def dd_add(a, b):
    s, e = two_sum(a[0], b[0])
    return quick_sum(s, e + (a[1] + b[1]))


def dd_mul(a, b):
    p, e = two_prod(a[0], *halves(a[0]), b[0], *halves(b[0]))
    return quick_sum(p, e + (a[0] * b[1] + a[1] * b[0]))


def dd_neg(a):
    return -a[0], -a[1]


def dd_over(a, b, inverse):
    q = a[0] * inverse
    rest = dd_add(a, dd_neg(dd_mul(b, (q, jnp.zeros_like(q)))))
    return quick_sum(q, rest[0] * inverse)


def row_sums(parts):
    rows = [jnp.sum(part, axis=0, keepdims=True) for part in parts]
    return jnp.concatenate(rows + [jnp.zeros_like(rows[0])], axis=0)


def precondition(pre_ref, u):
    return row_sums([pre_ref[i] * u[:F] for i in range(F)])


def gather(z, send_ref):
    cells = z.shape[1]
    tiles = cells // LANES
    source = [
        [jnp.broadcast_to(z[f : f + 1, t * LANES : (t + 1) * LANES], (8, LANES)) for t in range(tiles)]
        for f in range(F)
    ]
    taken = []
    for q in range(send_ref.shape[1] // 8):
        cell = send_ref[0, q * 8 : (q + 1) * 8, :]
        low = cell & (LANES - 1)
        high = cell >> 7
        taken.append([])
        for f in range(F):
            got = jnp.take_along_axis(source[f][0], low, axis=1, mode="promise_in_bounds")
            for t in range(1, tiles):
                other = jnp.take_along_axis(source[f][t], low, axis=1, mode="promise_in_bounds")
                got = jnp.where(high == t, other, got)
            taken[q].append(got)
    return taken


def mix(taken, coup_ref, halo_ref, msg_ref):
    peers = halo_ref.shape[1]
    lanes = lax.broadcasted_iota(jnp.int32, (8, LANES), 1)
    rows = lax.broadcasted_iota(jnp.int32, (8, peers), 0)
    cols = lax.broadcasted_iota(jnp.int32, (8, peers), 1)
    lens = jnp.broadcast_to(halo_ref[...], (8, peers))
    for q in range(peers // 8):
        size = jnp.sum(jnp.where(cols == rows + q * 8, lens, 0), axis=1, keepdims=True)
        live = lanes < size
        for i in range(F):
            total = coup_ref[0, i, 0, q * 8 : (q + 1) * 8, :] * taken[q][0]
            for j in range(1, F):
                total = total + coup_ref[0, i, j, q * 8 : (q + 1) * 8, :] * taken[q][j]
            msg_ref[pl.ds(q * 64 + i, 8, stride=8), :] = jnp.where(live, total, 0.0)
        msg_ref[pl.ds(q * 64 + F, 8, stride=8), :] = jnp.zeros((8, LANES), jnp.float32)


def scatter(recv_ref, cells_ref, tiles):
    peers = cells_ref.shape[1]
    spots = lax.broadcasted_iota(jnp.int32, (LANES, LANES), 0)
    left, right = [], []
    for s in range(peers):
        x = recv_ref[s * 8 : (s + 1) * 8, :]
        first = x.astype(jnp.bfloat16).astype(jnp.float32)
        rest = x - first
        second = rest.astype(jnp.bfloat16).astype(jnp.float32)
        third = rest - second
        cell = cells_ref[0, s : s + 1, :]
        low = jnp.broadcast_to(cell & (LANES - 1), (LANES, LANES))
        high = jnp.broadcast_to(cell >> 7, (8, LANES))
        pieces = []
        for t in range(tiles):
            here = high == t
            pieces += [jnp.where(here, part, 0.0) for part in (first, second, third)]
        left.append(jnp.concatenate(pieces, axis=0).astype(jnp.bfloat16))
        right.append(jnp.where(spots == low, 1.0, 0.0).astype(jnp.bfloat16))
    total = lax.dot_general(
        jnp.concatenate(left, axis=1),
        jnp.concatenate(right, axis=1),
        (((1,), (1,)), ((), ())),
        preferred_element_type=jnp.float32,
    )
    out = []
    for t in range(tiles):
        a, b, c = (total[t * 24 + 8 * k : t * 24 + 8 * k + 8] for k in range(3))
        out.append((c + b) + a)
    return jnp.concatenate(out, axis=1)


def local_part(z, diag_ref, low_ref, up_ref):
    cells = z.shape[1]
    col = lax.broadcasted_iota(jnp.int32, z.shape, 1)
    before = jnp.where(col == 0, 0.0, pltpu.roll(z, 1, 1))[:F]
    after = jnp.where(col == cells - 1, 0.0, pltpu.roll(z, cells - 1, 1))[:F]
    z = z[:F]
    return row_sums([diag_ref[i] * z + low_ref[i] * before + up_ref[i] * after for i in range(F)])


def products(us, last):
    cells = last.shape[1]
    tiles = [slice(t * LANES, (t + 1) * LANES) for t in range(cells // LANES)]
    lh, ll = halves(last)
    rows = lax.broadcasted_iota(jnp.int32, (8, LANES), 0)
    hi = jnp.zeros((8, LANES), jnp.float32)
    lo = jnp.zeros((8, LANES), jnp.float32)
    for i, u in enumerate(us):
        uh, ul = halves(u)
        terms = []
        for t in tiles:
            terms.append(two_prod(u[:, t], uh[:, t], ul[:, t], last[:, t], lh[:, t], ll[:, t]))
        while len(terms) > 1:
            terms = [dd_add(terms[k], terms[k + 1]) for k in range(0, len(terms), 2)]
        total = terms[0]
        for shift in (4, 2, 1):
            total = dd_add(total, tuple(pltpu.roll(v, shift, 0) for v in total))
        hi = jnp.where(rows == i, total[0], hi)
        lo = jnp.where(rows == i, total[1], lo)
    return hi, lo


def lane_sum(hi, lo):
    top = jnp.max(jnp.abs(hi), axis=1, keepdims=True) * 8192.0
    coarse = (hi + top) - top
    fine = (hi - coarse) + lo
    return quick_sum(jnp.sum(coarse, axis=1, keepdims=True), jnp.sum(fine, axis=1, keepdims=True))


def first_kernel(
    rhs_hbm, pre_hbm, coup_hbm, send_hbm, halo_hbm, diag_hbm, low_hbm, up_hbm, cells_hbm,
    u_ref, z_ref, msg_ref, y_ref, gram_ref, pre_ref, coup_ref, send_ref, halo_ref, diag_ref, low_ref, up_ref, cells_ref,
    rhs_ref, sems,
):
    whole = [(rhs_hbm, rhs_ref), (send_hbm, send_ref), (halo_hbm, halo_ref)]
    rows = [(pre_hbm.at[i], pre_ref.at[i]) for i in range(F)]
    faces = [(coup_hbm.at[0, i], coup_ref.at[0, i]) for i in range(F)]
    blocks = [(diag_hbm, diag_ref), (low_hbm, low_ref), (up_hbm, up_ref), (cells_hbm, cells_ref)]
    copies = [pltpu.make_async_copy(*pair, sems.at[k]) for k, pair in enumerate(whole + rows + faces + blocks)]
    for copy in copies:
        copy.start()
    for copy in copies[: len(whole) + F]:
        copy.wait()
    u = jnp.concatenate([rhs_ref[...], jnp.zeros((1, rhs_ref.shape[1]), jnp.float32)], axis=0)
    z = precondition(pre_ref, u)
    u_ref[...] = u
    z_ref[...] = z
    gram_ref[0], gram_ref[1] = products([u], u)
    taken = gather(z, send_ref)
    for copy in copies[len(whole) + F : len(whole) + 2 * F]:
        copy.wait()
    mix(taken, coup_ref, halo_ref, msg_ref)
    for copy in copies[len(whole) + 2 * F :]:
        copy.wait()
    y_ref[...] = local_part(z, diag_ref, low_ref, up_ref)


def step_kernel(col, recv_ref, cells_ref, y_ref, pre_ref, coup_ref, send_ref, halo_ref, diag_ref, low_ref, up_ref, *refs):
    u_refs, (u_ref, z_ref, msg_ref, next_ref, gram_ref) = refs[:col], refs[col:]
    u = y_ref[...] + scatter(recv_ref, cells_ref, y_ref.shape[1] // LANES)
    z = precondition(pre_ref, u)
    u_ref[...] = u
    z_ref[...] = z
    mix(gather(z, send_ref), coup_ref, halo_ref, msg_ref)
    next_ref[...] = local_part(z, diag_ref, low_ref, up_ref)
    gram_ref[0], gram_ref[1] = products([ref[...] for ref in u_refs] + [u], u)


def last_kernel(recv_ref, cells_ref, y_ref, *refs):
    u_refs, gram_refs, (u_ref, msg_ref) = refs[:ITERS], refs[ITERS : 2 * ITERS], refs[2 * ITERS :]
    u = y_ref[...] + scatter(recv_ref, cells_ref, y_ref.shape[1] // LANES)
    u_ref[...] = u
    columns = [(ref[0], ref[1]) for ref in gram_refs]
    columns.append(products([ref[...] for ref in u_refs] + [u], u))
    lane = lax.broadcasted_iota(jnp.int32, (8, LANES), 1)
    row = lax.broadcasted_iota(jnp.int32, (8, LANES), 0)
    placed = jnp.zeros((8, LANES), jnp.float32)
    for j in range(ITERS + 1):
        for part, total in enumerate(lane_sum(*columns[j])):
            placed = jnp.where(lane == row + (part * 64 + 8 * j), total, placed)
    placed = jnp.sum(placed, axis=0, keepdims=True)
    msg_ref[...] = jnp.broadcast_to(placed, msg_ref.shape)


def finish_kernel(count, got_ref, *refs):
    u_refs, z_refs = refs[: ITERS + 1], refs[ITERS + 1 : 2 * ITERS + 1]
    adj_ref, res_ref, flag_ref = refs[2 * ITERS + 1 :]
    lane = lax.broadcasted_iota(jnp.int32, (8, LANES), 1)
    rows = [got_ref[8 * k : 8 * k + 8, :] for k in range(count // 8)]
    pairs = [two_sum(rows[k], rows[k + 1]) for k in range(0, len(rows), 2)]
    while len(pairs) > 1:
        pairs = [dd_add(pairs[k], pairs[k + 1]) for k in range(0, len(pairs), 2)]
    total = pairs[0]
    for shift in (4, 2, 1):
        total = dd_add(total, tuple(pltpu.roll(v, shift, 0) for v in total))
    total = dd_add(total, tuple(pltpu.roll(v, 64, 1) for v in total))

    def entry(i, j):
        i, j = min(i, j), max(i, j)
        at = 8 * j + i
        return tuple(jnp.broadcast_to(v[0:1, at : at + 1], (1, LANES)) for v in total)

    n = ITERS
    mat = [[entry(i + 1, j + 1) if j >= i else None for j in range(n)] for i in range(n)]
    vec = [entry(0, i + 1) for i in range(n)]
    norms = [mat[i][i][0] for i in range(n)]
    first = entry(0, 0)
    ok = (first[0] > 1e-20) & (first[0] < 1e30)
    left = first
    scaled = [None] * n
    factor = [[None] * n for _ in range(n)]
    for k in range(n):
        pivot = mat[k][k]
        ok = ok & (norms[k] > 1e-20) & (norms[k] < 1e30) & (pivot[0] > 1e-9 * norms[k])
        inverse = 1.0 / pivot[0]
        scaled[k] = dd_over(vec[k], pivot, inverse)
        left = dd_add(left, dd_neg(dd_mul(vec[k], scaled[k])))
        for j in range(k + 1, n):
            factor[k][j] = dd_over(mat[k][j], pivot, inverse)
        for i in range(k + 1, n):
            for j in range(i, n):
                mat[i][j] = dd_add(mat[i][j], dd_neg(dd_mul(factor[k][i], mat[k][j])))
            vec[i] = dd_add(vec[i], dd_neg(dd_mul(factor[k][i], vec[k])))
    coef = [None] * n
    for k in reversed(range(n)):
        value = scaled[k]
        for j in range(k + 1, n):
            value = dd_add(value, dd_neg(dd_mul(factor[k][j], coef[j])))
        coef[k] = value
    reach = jnp.zeros((1, LANES), jnp.float32)
    for k in range(n):
        reach = reach + jnp.abs(coef[k][0]) * jnp.sqrt(norms[k])
    ok = ok & (reach * reach < 1e7 * left[0])
    flag_ref[0] = jnp.min(jnp.where(ok, 1, 0))
    cells = adj_ref.shape[1]
    weight = [jnp.broadcast_to(coef[k][0][:, :1], (8, cells)) for k in range(n)]
    adj = weight[0] * z_refs[0][...]
    res = u_refs[0][...] - weight[0] * u_refs[1][...]
    for k in range(1, n):
        adj = adj + weight[k] * z_refs[k][...]
        res = res - weight[k] * u_refs[k + 1][...]
    adj_ref[...] = adj[:F]
    res_ref[...] = res[:F]


def shape(*dims):
    return jax.ShapeDtypeStruct(dims, jnp.float32)


def call(kernel, out, *args, name, space=pltpu.VMEM, scratch=()):
    return pl.pallas_call(
        kernel,
        out_shape=out,
        name=name,
        in_specs=[pl.BlockSpec(memory_space=space)] * len(args),
        out_specs=tuple(
            pl.BlockSpec(memory_space=pltpu.SMEM if o.shape == (1,) else pltpu.VMEM) for o in out
        ),
        scratch_shapes=scratch,
        compiler_params=pltpu.CompilerParams(vmem_limit_bytes=24 * 2**20),
    )(*args)


def per_device(rhs, diag_blocks, lower_blocks, upper_blocks, precond, coupling, send_cells, recv_cells, halo_len):
    fields, cells = rhs.shape
    peers = send_cells.shape[1]
    count = peers * lax.axis_size("grp")
    vector = shape(8, cells)
    message = shape(peers * 8, LANES)
    args = (rhs, diag_blocks, lower_blocks, upper_blocks, precond, coupling, send_cells, recv_cells, halo_len)
    blocks = (diag_blocks, lower_blocks, upper_blocks)
    gram_shape = shape(2, 8, LANES)
    inputs = (precond, coupling, send_cells, halo_len, *blocks, recv_cells)
    u, z, msg, y, gram, *kept = call(
        first_kernel,
        (vector, vector, message, vector, gram_shape, *(jax.ShapeDtypeStruct(a.shape, a.dtype) for a in inputs)),
        rhs, *inputs,
        name="first",
        space=pltpu.HBM,
        scratch=(pltpu.VMEM(rhs.shape, jnp.float32), pltpu.SemaphoreType.DMA((2 * fields + 7,))),
    )
    face, blocks, recv_cells = kept[:4], kept[4:7], kept[7]
    us, zs, grams = [u], [z], [gram]
    for col in range(ITERS):
        got = lax.all_to_all(msg.reshape(peers, 8, LANES), "blk", 0, 0, tiled=True).reshape(peers * 8, LANES)
        if col < ITERS - 1:
            u, z, msg, y, gram = call(
                functools.partial(step_kernel, col + 1),
                (vector, vector, message, vector, gram_shape),
                got, recv_cells, y, *face, *blocks, *us,
                name="step",
            )
            zs.append(z)
            grams.append(gram)
        else:
            u, msg = call(last_kernel, (vector, shape(count, LANES)), got, recv_cells, y, *us, *grams, name="last")
        us.append(u)
    got = lax.all_to_all(msg, BOTH, 0, 0, tiled=True)
    adjoint, residual, flag = call(
        functools.partial(finish_kernel, count),
        (shape(fields, cells), shape(fields, cells), jax.ShapeDtypeStruct((1,), jnp.int32)),
        got, *us, *zs,
        name="finish",
    )
    args, adjoint, residual, flag = lax.optimization_barrier((args, adjoint, residual, flag))
    return lax.switch(flag[0], [lambda *_: arnoldi(*args), lambda *outs: outs], adjoint, residual)


def solution(mesh):
    return jax.shard_map(
        per_device,
        mesh=mesh,
        in_specs=(
            P(None, BOTH),
            P(None, None, BOTH),
            P(None, None, BOTH),
            P(None, None, BOTH),
            P(None, None, BOTH),
            P(BOTH, None, None, None, None),
            P(BOTH, None, None),
            P(BOTH, None, None),
            P(BOTH, None),
        ),
        out_specs=(P(None, BOTH), P(None, BOTH)),
        check_vma=False,
    )
```

```python
import functools

import jax
import jax.numpy as jnp
from jax import lax
from jax.experimental import pallas as pl
from jax.experimental.pallas import tpu as pltpu
from jax.sharding import PartitionSpec as P

ITERS = 4
F = 7
LANES = 128
BOTH = ("blk", "grp")


def mixing(blocks, field):
    total = blocks[:, 0] * field[0][None]
    for inner in range(1, field.shape[0]):
        total = total + blocks[:, inner] * field[inner][None]
    return total


def operate(field, diag_blocks, lower_blocks, upper_blocks, masked, send_flat, recv_flat):
    fields = field.shape[0]
    peers, width = masked.shape[2:]
    zero_col = jnp.zeros((fields, 1), jnp.float32)
    before = jnp.concatenate([zero_col, field[:, :-1]], axis=1)
    after = jnp.concatenate([field[:, 1:], zero_col], axis=1)
    outgoing = jnp.take(field, send_flat, axis=1).reshape(fields, peers, width)
    term = lax.all_to_all(mixing(masked, outgoing), "blk", split_axis=1, concat_axis=1, tiled=True)
    local = mixing(diag_blocks, field) + mixing(lower_blocks, before) + mixing(upper_blocks, after)
    return local.at[:, recv_flat].add(term.reshape(fields, -1))


def arnoldi(rhs, diag_blocks, lower_blocks, upper_blocks, precond, coupling, send_cells, recv_cells, halo_len):
    slots = jnp.arange(coupling.shape[4], dtype=jnp.int32)
    live = (slots[None, :] < halo_len[0][:, None]).astype(jnp.float32)
    masked = coupling[0] * live[None, None, :, :]
    send_flat = send_cells[0].reshape(-1)
    recv_flat = recv_cells[0].reshape(-1)

    def apply_op(field):
        return operate(field, diag_blocks, lower_blocks, upper_blocks, masked, send_flat, recv_flat)

    beta = jnp.sqrt(lax.psum(jnp.sum(rhs * rhs), BOTH))
    basis = [rhs / beta]
    hess = jnp.zeros((ITERS + 1, ITERS), jnp.float32)
    for col in range(ITERS):
        product = apply_op(mixing(precond, basis[col]))
        proj = lax.psum(jnp.stack([jnp.sum(vector * product) for vector in basis]), BOTH)
        remain = product
        for index in range(col + 1):
            remain = remain - proj[index] * basis[index]
        height = jnp.sqrt(lax.psum(jnp.sum(remain * remain), BOTH))
        hess = hess.at[: col + 1, col].set(proj).at[col + 1, col].set(height)
        basis.append(remain / height)
    gram = jnp.dot(hess.T, hess, precision=lax.Precision.HIGHEST)
    factor = jnp.linalg.cholesky(gram)
    coef = jax.scipy.linalg.cho_solve((factor, True), beta * hess[0])
    combo = coef[0] * basis[0]
    for index in range(1, ITERS):
        combo = combo + coef[index] * basis[index]
    adjoint = mixing(precond, combo)
    return adjoint, rhs - apply_op(adjoint)


def two_sum(a, b):
    s = a + b
    t = s - a
    return s, (a - (s - t)) + (b - t)


def quick_sum(a, b):
    s = a + b
    return s, b - (s - a)


def halves(a):
    t = a * 4097.0
    high = t - (t - a)
    return high, a - high


def two_prod(a, ah, al, b, bh, bl):
    p = a * b
    return p, ((ah * bh - p) + ah * bl + al * bh) + al * bl


def dd_add(a, b):
    s, e = two_sum(a[0], b[0])
    return quick_sum(s, e + (a[1] + b[1]))


def dd_mul(a, b):
    p, e = two_prod(a[0], *halves(a[0]), b[0], *halves(b[0]))
    return quick_sum(p, e + (a[0] * b[1] + a[1] * b[0]))


def dd_neg(a):
    return -a[0], -a[1]


def dd_over(a, b, inverse):
    q = a[0] * inverse
    rest = dd_add(a, dd_neg(dd_mul(b, (q, jnp.zeros_like(q)))))
    return quick_sum(q, rest[0] * inverse)


def row_sums(parts):
    rows = [jnp.sum(part, axis=0, keepdims=True) for part in parts]
    return jnp.concatenate(rows + [jnp.zeros_like(rows[0])], axis=0)


def precondition(pre_ref, u):
    return row_sums([pre_ref[i] * u[:F] for i in range(F)])


def gather(z, send_ref):
    cells = z.shape[1]
    tiles = cells // LANES
    source = [
        [jnp.broadcast_to(z[f : f + 1, t * LANES : (t + 1) * LANES], (8, LANES)) for t in range(tiles)]
        for f in range(F)
    ]
    taken = []
    for q in range(send_ref.shape[1] // 8):
        cell = send_ref[0, q * 8 : (q + 1) * 8, :]
        low = cell & (LANES - 1)
        high = cell >> 7
        taken.append([])
        for f in range(F):
            got = jnp.take_along_axis(source[f][0], low, axis=1, mode="promise_in_bounds")
            for t in range(1, tiles):
                other = jnp.take_along_axis(source[f][t], low, axis=1, mode="promise_in_bounds")
                got = jnp.where(high == t, other, got)
            taken[q].append(got)
    return taken


def mix(taken, coup_ref, halo_ref, msg_ref):
    peers = halo_ref.shape[1]
    lanes = lax.broadcasted_iota(jnp.int32, (8, LANES), 1)
    rows = lax.broadcasted_iota(jnp.int32, (8, peers), 0)
    cols = lax.broadcasted_iota(jnp.int32, (8, peers), 1)
    lens = jnp.broadcast_to(halo_ref[...], (8, peers))
    for q in range(peers // 8):
        size = jnp.sum(jnp.where(cols == rows + q * 8, lens, 0), axis=1, keepdims=True)
        live = lanes < size
        for i in range(F):
            total = coup_ref[0, i, 0, q * 8 : (q + 1) * 8, :] * taken[q][0]
            for j in range(1, F):
                total = total + coup_ref[0, i, j, q * 8 : (q + 1) * 8, :] * taken[q][j]
            msg_ref[pl.ds(q * 64 + i, 8, stride=8), :] = jnp.where(live, total, 0.0)
        msg_ref[pl.ds(q * 64 + F, 8, stride=8), :] = jnp.zeros((8, LANES), jnp.float32)


def scatter(recv_ref, cells_ref, tiles):
    peers = cells_ref.shape[1]
    spots = lax.broadcasted_iota(jnp.int32, (LANES, LANES), 0)
    left, right = [], []
    for s in range(peers):
        x = recv_ref[s * 8 : (s + 1) * 8, :]
        first = x.astype(jnp.bfloat16).astype(jnp.float32)
        second = x - first
        cell = cells_ref[0, s : s + 1, :]
        low = jnp.broadcast_to(cell & (LANES - 1), (LANES, LANES))
        high = jnp.broadcast_to(cell >> 7, (8, LANES))
        pieces = []
        for t in range(tiles):
            here = high == t
            pieces += [jnp.where(here, part, 0.0) for part in (first, second)]
        left.append(jnp.concatenate(pieces, axis=0).astype(jnp.bfloat16))
        right.append(jnp.where(spots == low, 1.0, 0.0).astype(jnp.bfloat16))
    total = lax.dot_general(
        jnp.concatenate(left, axis=1),
        jnp.concatenate(right, axis=1),
        (((1,), (1,)), ((), ())),
        preferred_element_type=jnp.float32,
    )
    out = []
    for t in range(tiles):
        out.append(total[t * 16 : t * 16 + 8] + total[t * 16 + 8 : t * 16 + 16])
    return jnp.concatenate(out, axis=1)


def local_part(z, diag_ref, low_ref, up_ref):
    cells = z.shape[1]
    col = lax.broadcasted_iota(jnp.int32, z.shape, 1)
    before = jnp.where(col == 0, 0.0, pltpu.roll(z, 1, 1))[:F]
    after = jnp.where(col == cells - 1, 0.0, pltpu.roll(z, cells - 1, 1))[:F]
    z = z[:F]
    return row_sums([diag_ref[i] * z + low_ref[i] * before + up_ref[i] * after for i in range(F)])


def products(us, last):
    cells = last.shape[1]
    tiles = [slice(t * LANES, (t + 1) * LANES) for t in range(cells // LANES)]
    lh, ll = halves(last)
    rows = lax.broadcasted_iota(jnp.int32, (8, LANES), 0)
    hi = jnp.zeros((8, LANES), jnp.float32)
    lo = jnp.zeros((8, LANES), jnp.float32)
    for i, u in enumerate(us):
        uh, ul = halves(u)
        terms = []
        for t in tiles:
            terms.append(two_prod(u[:, t], uh[:, t], ul[:, t], last[:, t], lh[:, t], ll[:, t]))
        while len(terms) > 1:
            terms = [dd_add(terms[k], terms[k + 1]) for k in range(0, len(terms), 2)]
        total = terms[0]
        for shift in (4, 2, 1):
            total = dd_add(total, tuple(pltpu.roll(v, shift, 0) for v in total))
        hi = jnp.where(rows == i, total[0], hi)
        lo = jnp.where(rows == i, total[1], lo)
    return hi, lo


def lane_sum(hi, lo):
    top = jnp.max(jnp.abs(hi), axis=1, keepdims=True) * 8192.0
    coarse = (hi + top) - top
    fine = (hi - coarse) + lo
    return quick_sum(jnp.sum(coarse, axis=1, keepdims=True), jnp.sum(fine, axis=1, keepdims=True))


def first_kernel(
    rhs_hbm, pre_hbm, coup_hbm, send_hbm, halo_hbm, diag_hbm, low_hbm, up_hbm, cells_hbm,
    u_ref, z_ref, msg_ref, y_ref, gram_ref, pre_ref, coup_ref, send_ref, halo_ref, diag_ref, low_ref, up_ref, cells_ref,
    rhs_ref, sems,
):
    whole = [(rhs_hbm, rhs_ref), (send_hbm, send_ref), (halo_hbm, halo_ref)]
    rows = [(pre_hbm, pre_ref)]
    faces = [(coup_hbm, coup_ref)]
    blocks = [(diag_hbm, diag_ref), (low_hbm, low_ref), (up_hbm, up_ref), (cells_hbm, cells_ref)]
    copies = [pltpu.make_async_copy(*pair, sems.at[k]) for k, pair in enumerate(whole + rows + faces + blocks)]
    for copy in copies:
        copy.start()
    for copy in copies[: len(whole)]:
        copy.wait()
    u = jnp.concatenate([rhs_ref[...], jnp.zeros((1, rhs_ref.shape[1]), jnp.float32)], axis=0)
    u_ref[...] = u
    gram_ref[0], gram_ref[1] = products([u], u)
    for copy in copies[len(whole) : len(whole) + 1]:
        copy.wait()
    z = precondition(pre_ref, u)
    z_ref[...] = z
    taken = gather(z, send_ref)
    for copy in copies[len(whole) + 1 : len(whole) + 2]:
        copy.wait()
    mix(taken, coup_ref, halo_ref, msg_ref)
    for copy in copies[len(whole) + 2 :]:
        copy.wait()
    y_ref[...] = local_part(z, diag_ref, low_ref, up_ref)


def step_kernel(col, recv_ref, cells_ref, y_ref, pre_ref, coup_ref, send_ref, halo_ref, diag_ref, low_ref, up_ref, *refs):
    u_refs, (u_ref, z_ref, msg_ref, next_ref, gram_ref) = refs[:col], refs[col:]
    u = y_ref[...] + scatter(recv_ref, cells_ref, y_ref.shape[1] // LANES)
    z = precondition(pre_ref, u)
    u_ref[...] = u
    z_ref[...] = z
    mix(gather(z, send_ref), coup_ref, halo_ref, msg_ref)
    next_ref[...] = local_part(z, diag_ref, low_ref, up_ref)
    gram_ref[0], gram_ref[1] = products([ref[...] for ref in u_refs] + [u], u)


def last_kernel(recv_ref, cells_ref, y_ref, *refs):
    u_refs, gram_refs, (u_ref, msg_ref) = refs[:ITERS], refs[ITERS : 2 * ITERS], refs[2 * ITERS :]
    u = y_ref[...] + scatter(recv_ref, cells_ref, y_ref.shape[1] // LANES)
    u_ref[...] = u
    columns = [(ref[0], ref[1]) for ref in gram_refs]
    columns.append(products([ref[...] for ref in u_refs] + [u], u))
    lane = lax.broadcasted_iota(jnp.int32, (8, LANES), 1)
    row = lax.broadcasted_iota(jnp.int32, (8, LANES), 0)
    placed = jnp.zeros((8, LANES), jnp.float32)
    for j in range(ITERS + 1):
        for part, total in enumerate(lane_sum(*columns[j])):
            placed = jnp.where(lane == row + (part * 64 + 8 * j), total, placed)
    placed = jnp.sum(placed, axis=0, keepdims=True)
    msg_ref[...] = jnp.broadcast_to(placed, msg_ref.shape)


def finish_kernel(count, got_ref, *refs):
    u_refs, z_refs = refs[: ITERS + 1], refs[ITERS + 1 : 2 * ITERS + 1]
    adj_ref, res_ref, flag_ref = refs[2 * ITERS + 1 :]
    lane = lax.broadcasted_iota(jnp.int32, (8, LANES), 1)
    rows = [got_ref[8 * k : 8 * k + 8, :] for k in range(count // 8)]
    pairs = [two_sum(rows[k], rows[k + 1]) for k in range(0, len(rows), 2)]
    while len(pairs) > 1:
        pairs = [dd_add(pairs[k], pairs[k + 1]) for k in range(0, len(pairs), 2)]
    total = pairs[0]
    for shift in (4, 2, 1):
        total = dd_add(total, tuple(pltpu.roll(v, shift, 0) for v in total))
    total = dd_add(total, tuple(pltpu.roll(v, 64, 1) for v in total))

    def entry(i, j):
        i, j = min(i, j), max(i, j)
        at = 8 * j + i
        return tuple(jnp.broadcast_to(v[0:1, at : at + 1], (1, LANES)) for v in total)

    n = ITERS
    mat = [[entry(i + 1, j + 1) if j >= i else None for j in range(n)] for i in range(n)]
    vec = [entry(0, i + 1) for i in range(n)]
    norms = [mat[i][i][0] for i in range(n)]
    first = entry(0, 0)
    ok = (first[0] > 1e-20) & (first[0] < 1e30)
    left = first
    scaled = [None] * n
    factor = [[None] * n for _ in range(n)]
    for k in range(n):
        pivot = mat[k][k]
        ok = ok & (norms[k] > 1e-20) & (norms[k] < 1e30) & (pivot[0] > 1e-9 * norms[k])
        inverse = 1.0 / pivot[0]
        scaled[k] = dd_over(vec[k], pivot, inverse)
        left = dd_add(left, dd_neg(dd_mul(vec[k], scaled[k])))
        for j in range(k + 1, n):
            factor[k][j] = dd_over(mat[k][j], pivot, inverse)
        for i in range(k + 1, n):
            for j in range(i, n):
                mat[i][j] = dd_add(mat[i][j], dd_neg(dd_mul(factor[k][i], mat[k][j])))
            vec[i] = dd_add(vec[i], dd_neg(dd_mul(factor[k][i], vec[k])))
    coef = [None] * n
    for k in reversed(range(n)):
        value = scaled[k]
        for j in range(k + 1, n):
            value = dd_add(value, dd_neg(dd_mul(factor[k][j], coef[j])))
        coef[k] = value
    reach = jnp.zeros((1, LANES), jnp.float32)
    for k in range(n):
        reach = reach + jnp.abs(coef[k][0]) * jnp.sqrt(norms[k])
    ok = ok & (reach * reach < 1e7 * left[0])
    flag_ref[...] = jnp.where(ok, 1, 0)
    cells = adj_ref.shape[1]
    weight = [jnp.broadcast_to(coef[k][0][:, :1], (8, cells)) for k in range(n)]
    adj = weight[0] * z_refs[0][...]
    res = u_refs[0][...] - weight[0] * u_refs[1][...]
    for k in range(1, n):
        adj = adj + weight[k] * z_refs[k][...]
        res = res - weight[k] * u_refs[k + 1][...]
    adj_ref[...] = adj[:F]
    res_ref[...] = res[:F]


def shape(*dims):
    return jax.ShapeDtypeStruct(dims, jnp.float32)


def call(kernel, out, *args, name, space=pltpu.VMEM, scratch=()):
    return pl.pallas_call(
        kernel,
        out_shape=out,
        name=name,
        in_specs=[pl.BlockSpec(memory_space=space)] * len(args),
        out_specs=tuple(
            pl.BlockSpec(memory_space=pltpu.SMEM if o.shape == (1,) else pltpu.VMEM) for o in out
        ),
        scratch_shapes=scratch,
        compiler_params=pltpu.CompilerParams(vmem_limit_bytes=24 * 2**20),
    )(*args)


def per_device(rhs, diag_blocks, lower_blocks, upper_blocks, precond, coupling, send_cells, recv_cells, halo_len):
    fields, cells = rhs.shape
    peers = send_cells.shape[1]
    count = peers * lax.axis_size("grp")
    vector = shape(8, cells)
    message = shape(peers * 8, LANES)
    args = (rhs, diag_blocks, lower_blocks, upper_blocks, precond, coupling, send_cells, recv_cells, halo_len)
    blocks = (diag_blocks, lower_blocks, upper_blocks)
    gram_shape = shape(2, 8, LANES)
    inputs = (precond, coupling, send_cells, halo_len, *blocks, recv_cells)
    u, z, msg, y, gram, *kept = call(
        first_kernel,
        (vector, vector, message, vector, gram_shape, *(jax.ShapeDtypeStruct(a.shape, a.dtype) for a in inputs)),
        rhs, *inputs,
        name="first",
        space=pltpu.HBM,
        scratch=(pltpu.VMEM(rhs.shape, jnp.float32), pltpu.SemaphoreType.DMA((2 * fields + 7,))),
    )
    face, blocks, recv_cells = kept[:4], kept[4:7], kept[7]
    us, zs, grams = [u], [z], [gram]
    for col in range(ITERS):
        got = lax.all_to_all(msg.reshape(peers, 8, LANES), "blk", 0, 0, tiled=True).reshape(peers * 8, LANES)
        if col < ITERS - 1:
            u, z, msg, y, gram = call(
                functools.partial(step_kernel, col + 1),
                (vector, vector, message, vector, gram_shape),
                got, recv_cells, y, *face, *blocks, *us,
                name="step",
            )
            zs.append(z)
            grams.append(gram)
        else:
            u, msg = call(last_kernel, (vector, shape(count, LANES)), got, recv_cells, y, *us, *grams, name="last")
        us.append(u)
    got = lax.all_to_all(msg, BOTH, 0, 0, tiled=True)
    adjoint, residual, flag = call(
        functools.partial(finish_kernel, count),
        (shape(fields, cells), shape(fields, cells), jax.ShapeDtypeStruct((1, LANES), jnp.int32)),
        got, *us, *zs,
        name="finish",
    )
    args, adjoint, residual, flag = lax.optimization_barrier((args, adjoint, residual, flag))
    return lax.switch(flag[0, 0], [lambda *_: arnoldi(*args), lambda *outs: outs], adjoint, residual)


def solution(mesh):
    return jax.shard_map(
        per_device,
        mesh=mesh,
        in_specs=(
            P(None, BOTH),
            P(None, None, BOTH),
            P(None, None, BOTH),
            P(None, None, BOTH),
            P(None, None, BOTH),
            P(BOTH, None, None, None, None),
            P(BOTH, None, None),
            P(BOTH, None, None),
            P(BOTH, None),
        ),
        out_specs=(P(None, BOTH), P(None, BOTH)),
        check_vma=False,
    )
```

```python
import functools
import math

import jax
import jax.numpy as jnp
from jax import lax
from jax.experimental import pallas as pl
from jax.experimental.pallas import tpu as pltpu
from jax.sharding import PartitionSpec as P

ITERS = 4
F = 7
LANES = 128
BOTH = ("blk", "grp")


def mixing(blocks, field):
    total = blocks[:, 0] * field[0][None]
    for inner in range(1, field.shape[0]):
        total = total + blocks[:, inner] * field[inner][None]
    return total


def operate(field, diag_blocks, lower_blocks, upper_blocks, masked, send_flat, recv_flat):
    fields = field.shape[0]
    peers, width = masked.shape[2:]
    zero_col = jnp.zeros((fields, 1), jnp.float32)
    before = jnp.concatenate([zero_col, field[:, :-1]], axis=1)
    after = jnp.concatenate([field[:, 1:], zero_col], axis=1)
    outgoing = jnp.take(field, send_flat, axis=1).reshape(fields, peers, width)
    term = lax.all_to_all(mixing(masked, outgoing), "blk", split_axis=1, concat_axis=1, tiled=True)
    local = mixing(diag_blocks, field) + mixing(lower_blocks, before) + mixing(upper_blocks, after)
    return local.at[:, recv_flat].add(term.reshape(fields, -1))


def arnoldi(rhs, diag_blocks, lower_blocks, upper_blocks, precond, coupling, send_cells, recv_cells, halo_len):
    slots = jnp.arange(coupling.shape[4], dtype=jnp.int32)
    live = (slots[None, :] < halo_len[0][:, None]).astype(jnp.float32)
    masked = coupling[0] * live[None, None, :, :]
    send_flat = send_cells[0].reshape(-1)
    recv_flat = recv_cells[0].reshape(-1)

    def apply_op(field):
        return operate(field, diag_blocks, lower_blocks, upper_blocks, masked, send_flat, recv_flat)

    beta = jnp.sqrt(lax.psum(jnp.sum(rhs * rhs), BOTH))
    basis = [rhs / beta]
    hess = jnp.zeros((ITERS + 1, ITERS), jnp.float32)
    for col in range(ITERS):
        product = apply_op(mixing(precond, basis[col]))
        proj = lax.psum(jnp.stack([jnp.sum(vector * product) for vector in basis]), BOTH)
        remain = product
        for index in range(col + 1):
            remain = remain - proj[index] * basis[index]
        height = jnp.sqrt(lax.psum(jnp.sum(remain * remain), BOTH))
        hess = hess.at[: col + 1, col].set(proj).at[col + 1, col].set(height)
        basis.append(remain / height)
    gram = jnp.dot(hess.T, hess, precision=lax.Precision.HIGHEST)
    factor = jnp.linalg.cholesky(gram)
    coef = jax.scipy.linalg.cho_solve((factor, True), beta * hess[0])
    combo = coef[0] * basis[0]
    for index in range(1, ITERS):
        combo = combo + coef[index] * basis[index]
    adjoint = mixing(precond, combo)
    return adjoint, rhs - apply_op(adjoint)


def two_sum(a, b):
    s = a + b
    t = s - a
    return s, (a - (s - t)) + (b - t)


def quick_sum(a, b):
    s = a + b
    return s, b - (s - a)


def halves(a):
    t = a * 4097.0
    high = t - (t - a)
    return high, a - high


def two_prod(a, ah, al, b, bh, bl):
    p = a * b
    return p, ((ah * bh - p) + ah * bl + al * bh) + al * bl


def dd_add(a, b):
    s, e = two_sum(a[0], b[0])
    return quick_sum(s, e + (a[1] + b[1]))


def dd_mul(a, b):
    p, e = two_prod(a[0], *halves(a[0]), b[0], *halves(b[0]))
    return quick_sum(p, e + (a[0] * b[1] + a[1] * b[0]))


def dd_neg(a):
    return -a[0], -a[1]


def dd_over(a, b, inverse):
    q = a[0] * inverse
    rest = dd_add(a, dd_neg(dd_mul(b, (q, jnp.zeros_like(q)))))
    return quick_sum(q, rest[0] * inverse)


def row_sums(parts):
    rows = [jnp.sum(part, axis=0, keepdims=True) for part in parts]
    return jnp.concatenate(rows + [jnp.zeros_like(rows[0])], axis=0)


def precondition(pre_ref, u):
    return row_sums([pre_ref[i] * u[:F] for i in range(F)])


def gather(z, send_ref):
    cells = z.shape[1]
    tiles = cells // LANES
    source = [
        [jnp.broadcast_to(z[f : f + 1, t * LANES : (t + 1) * LANES], (8, LANES)) for t in range(tiles)]
        for f in range(F)
    ]
    taken = []
    for q in range(send_ref.shape[1] // 8):
        cell = send_ref[0, q * 8 : (q + 1) * 8, :]
        low = cell & (LANES - 1)
        high = cell >> 7
        taken.append([])
        for f in range(F):
            got = jnp.take_along_axis(source[f][0], low, axis=1, mode="promise_in_bounds")
            for t in range(1, tiles):
                other = jnp.take_along_axis(source[f][t], low, axis=1, mode="promise_in_bounds")
                got = jnp.where(high == t, other, got)
            taken[q].append(got)
    return taken


def mix(taken, coup_ref, halo_ref, msg_ref):
    peers = halo_ref.shape[1]
    lanes = lax.broadcasted_iota(jnp.int32, (8, LANES), 1)
    rows = lax.broadcasted_iota(jnp.int32, (8, peers), 0)
    cols = lax.broadcasted_iota(jnp.int32, (8, peers), 1)
    lens = jnp.broadcast_to(halo_ref[...], (8, peers))
    for q in range(peers // 8):
        size = jnp.sum(jnp.where(cols == rows + q * 8, lens, 0), axis=1, keepdims=True)
        live = lanes < size
        for i in range(F):
            total = coup_ref[0, i, 0, q * 8 : (q + 1) * 8, :] * taken[q][0]
            for j in range(1, F):
                total = total + coup_ref[0, i, j, q * 8 : (q + 1) * 8, :] * taken[q][j]
            msg_ref[pl.ds(q * 64 + i, 8, stride=8), :] = jnp.where(live, total, 0.0)
        msg_ref[pl.ds(q * 64 + F, 8, stride=8), :] = jnp.zeros((8, LANES), jnp.float32)


def scatter(recv_ref, cells_ref, tiles):
    peers = cells_ref.shape[1]
    spots = lax.broadcasted_iota(jnp.int32, (LANES, LANES), 0)
    left, right = [], []
    for s in range(peers):
        x = recv_ref[s * 8 : (s + 1) * 8, :]
        first = x.astype(jnp.bfloat16).astype(jnp.float32)
        second = x - first
        cell = cells_ref[0, s : s + 1, :]
        low = jnp.broadcast_to(cell & (LANES - 1), (LANES, LANES))
        high = jnp.broadcast_to(cell >> 7, (8, LANES))
        pieces = []
        for t in range(tiles):
            here = high == t
            pieces += [jnp.where(here, part, 0.0) for part in (first, second)]
        left.append(jnp.concatenate(pieces, axis=0).astype(jnp.bfloat16))
        right.append(jnp.where(spots == low, 1.0, 0.0).astype(jnp.bfloat16))
    total = lax.dot_general(
        jnp.concatenate(left, axis=1),
        jnp.concatenate(right, axis=1),
        (((1,), (1,)), ((), ())),
        preferred_element_type=jnp.float32,
    )
    out = []
    for t in range(tiles):
        out.append(total[t * 16 : t * 16 + 8] + total[t * 16 + 8 : t * 16 + 16])
    return jnp.concatenate(out, axis=1)


def local_part(z, diag_ref, low_ref, up_ref):
    cells = z.shape[1]
    col = lax.broadcasted_iota(jnp.int32, z.shape, 1)
    before = jnp.where(col == 0, 0.0, pltpu.roll(z, 1, 1))[:F]
    after = jnp.where(col == cells - 1, 0.0, pltpu.roll(z, cells - 1, 1))[:F]
    z = z[:F]
    return row_sums([diag_ref[i] * z + low_ref[i] * before + up_ref[i] * after for i in range(F)])


def products(us, last):
    cells = last.shape[1]
    tiles = [slice(t * LANES, (t + 1) * LANES) for t in range(cells // LANES)]
    lh, ll = halves(last)
    rows = lax.broadcasted_iota(jnp.int32, (8, LANES), 0)
    hi = jnp.zeros((8, LANES), jnp.float32)
    lo = jnp.zeros((8, LANES), jnp.float32)
    for i, u in enumerate(us):
        uh, ul = halves(u)
        terms = []
        for t in tiles:
            terms.append(two_prod(u[:, t], uh[:, t], ul[:, t], last[:, t], lh[:, t], ll[:, t]))
        while len(terms) > 1:
            terms = [dd_add(terms[k], terms[k + 1]) for k in range(0, len(terms), 2)]
        total = terms[0]
        for shift in (4, 2, 1):
            total = dd_add(total, tuple(pltpu.roll(v, shift, 0) for v in total))
        hi = jnp.where(rows == i, total[0], hi)
        lo = jnp.where(rows == i, total[1], lo)
    return hi, lo


def lane_sum(hi, lo):
    top = jnp.max(jnp.abs(hi), axis=1, keepdims=True) * 8192.0
    coarse = (hi + top) - top
    fine = (hi - coarse) + lo
    return quick_sum(jnp.sum(coarse, axis=1, keepdims=True), jnp.sum(fine, axis=1, keepdims=True))


def first_kernel(
    rhs_hbm, pre_hbm, coup_hbm, send_hbm, halo_hbm, diag_hbm, low_hbm, up_hbm, cells_hbm,
    u_ref, z_ref, msg_ref, y_ref, gram_ref, pre_ref, coup_ref, send_ref, halo_ref, diag_ref, low_ref, up_ref, cells_ref,
    rhs_ref, sems,
):
    whole = [(rhs_hbm, rhs_ref), (send_hbm, send_ref), (halo_hbm, halo_ref)]
    rows = [(pre_hbm, pre_ref)]
    faces = [(coup_hbm, coup_ref)]
    blocks = [(diag_hbm, diag_ref), (low_hbm, low_ref), (up_hbm, up_ref), (cells_hbm, cells_ref)]
    copies = [pltpu.make_async_copy(*pair, sems.at[k]) for k, pair in enumerate(whole + rows + faces + blocks)]
    for copy in copies:
        copy.start()
    for copy in copies[: len(whole)]:
        copy.wait()
    u = jnp.concatenate([rhs_ref[...], jnp.zeros((1, rhs_ref.shape[1]), jnp.float32)], axis=0)
    u_ref[...] = u
    gram_ref[0], gram_ref[1] = products([u], u)
    for copy in copies[len(whole) : len(whole) + 1]:
        copy.wait()
    z = precondition(pre_ref, u)
    z_ref[...] = z
    taken = gather(z, send_ref)
    for copy in copies[len(whole) + 1 : len(whole) + 2]:
        copy.wait()
    mix(taken, coup_ref, halo_ref, msg_ref)
    for copy in copies[len(whole) + 2 :]:
        copy.wait()
    y_ref[...] = local_part(z, diag_ref, low_ref, up_ref)


def step_kernel(col, recv_ref, cells_ref, y_ref, pre_ref, coup_ref, send_ref, halo_ref, diag_ref, low_ref, up_ref, *refs):
    u_refs, (u_ref, z_ref, msg_ref, next_ref, gram_ref) = refs[:col], refs[col:]
    u = y_ref[...] + scatter(recv_ref, cells_ref, y_ref.shape[1] // LANES)
    z = precondition(pre_ref, u)
    u_ref[...] = u
    z_ref[...] = z
    mix(gather(z, send_ref), coup_ref, halo_ref, msg_ref)
    next_ref[...] = local_part(z, diag_ref, low_ref, up_ref)
    gram_ref[0], gram_ref[1] = products([ref[...] for ref in u_refs] + [u], u)


def last_kernel(recv_ref, cells_ref, y_ref, *refs):
    u_refs, gram_refs, (u_ref, row_ref) = refs[:ITERS], refs[ITERS : 2 * ITERS], refs[2 * ITERS :]
    u = y_ref[...] + scatter(recv_ref, cells_ref, y_ref.shape[1] // LANES)
    u_ref[...] = u
    columns = [(ref[0], ref[1]) for ref in gram_refs]
    columns.append(products([ref[...] for ref in u_refs] + [u], u))
    lane = lax.broadcasted_iota(jnp.int32, (8, LANES), 1)
    row = lax.broadcasted_iota(jnp.int32, (8, LANES), 0)
    placed = jnp.zeros((8, LANES), jnp.float32)
    for j in range(ITERS + 1):
        for part, total in enumerate(lane_sum(*columns[j])):
            placed = jnp.where(lane == row + (part * 64 + 8 * j), total, placed)
    row_ref[...] = jnp.broadcast_to(jnp.sum(placed, axis=0, keepdims=True), row_ref.shape)


def pair_kernel(own_ref, other_ref, msg_ref):
    total, error = two_sum(own_ref[...], other_ref[...])
    lane = lax.broadcasted_iota(jnp.int32, total.shape, 1)
    row = jnp.where(lane < 64, total, total + pltpu.roll(error, 64, 1))
    msg_ref[...] = jnp.concatenate([row] * (msg_ref.shape[0] // 8), axis=0)


def finish_kernel(count, got_ref, *refs):
    u_refs, z_refs = refs[: ITERS + 1], refs[ITERS + 1 : 2 * ITERS + 1]
    adj_ref, res_ref, flag_ref = refs[2 * ITERS + 1 :]
    lane = lax.broadcasted_iota(jnp.int32, (8, LANES), 1)
    rows = [got_ref[8 * k : 8 * k + 8, :] for k in range(count // 8)]
    pairs = [two_sum(rows[k], rows[k + 1]) for k in range(0, len(rows), 2)]
    while len(pairs) > 1:
        pairs = [dd_add(pairs[k], pairs[k + 1]) for k in range(0, len(pairs), 2)]
    total = pairs[0]
    for shift in (4, 2, 1):
        total = dd_add(total, tuple(pltpu.roll(v, shift, 0) for v in total))
    total = dd_add(total, tuple(pltpu.roll(v, 64, 1) for v in total))

    def entry(i, j):
        i, j = min(i, j), max(i, j)
        at = 8 * j + i
        return tuple(jnp.broadcast_to(v[0:1, at : at + 1], (1, LANES)) for v in total)

    n = ITERS
    mat = [[entry(i + 1, j + 1) if j >= i else None for j in range(n)] for i in range(n)]
    vec = [entry(0, i + 1) for i in range(n)]
    norms = [mat[i][i][0] for i in range(n)]
    first = entry(0, 0)
    ok = (first[0] > 1e-20) & (first[0] < 1e30)
    left = first
    scaled = [None] * n
    factor = [[None] * n for _ in range(n)]
    for k in range(n):
        pivot = mat[k][k]
        ok = ok & (norms[k] > 1e-20) & (norms[k] < 1e30) & (pivot[0] > 1e-9 * norms[k])
        inverse = 1.0 / pivot[0]
        scaled[k] = dd_over(vec[k], pivot, inverse)
        left = dd_add(left, dd_neg(dd_mul(vec[k], scaled[k])))
        for j in range(k + 1, n):
            factor[k][j] = dd_over(mat[k][j], pivot, inverse)
        for i in range(k + 1, n):
            for j in range(i, n):
                mat[i][j] = dd_add(mat[i][j], dd_neg(dd_mul(factor[k][i], mat[k][j])))
            vec[i] = dd_add(vec[i], dd_neg(dd_mul(factor[k][i], vec[k])))
    coef = [None] * n
    for k in reversed(range(n)):
        value = scaled[k]
        for j in range(k + 1, n):
            value = dd_add(value, dd_neg(dd_mul(factor[k][j], coef[j])))
        coef[k] = value
    reach = jnp.zeros((1, LANES), jnp.float32)
    for k in range(n):
        reach = reach + jnp.abs(coef[k][0]) * jnp.sqrt(norms[k])
    ok = ok & (reach * reach < 1e7 * left[0])
    flag_ref[...] = jnp.where(ok, 1, 0)
    cells = adj_ref.shape[1]
    weight = [jnp.broadcast_to(coef[k][0][:, :1], (8, cells)) for k in range(n)]
    adj = weight[0] * z_refs[0][...]
    res = u_refs[0][...] - weight[0] * u_refs[1][...]
    for k in range(1, n):
        adj = adj + weight[k] * z_refs[k][...]
        res = res - weight[k] * u_refs[k + 1][...]
    adj_ref[...] = adj[:F]
    res_ref[...] = res[:F]


def shape(*dims):
    return jax.ShapeDtypeStruct(dims, jnp.float32)


def call(kernel, out, *args, name, space=pltpu.VMEM, scratch=()):
    return pl.pallas_call(
        kernel,
        out_shape=out,
        name=name,
        in_specs=[pl.BlockSpec(memory_space=space)] * len(args),
        out_specs=tuple(
            pl.BlockSpec(memory_space=pltpu.SMEM if o.shape == (1,) else pltpu.VMEM) for o in out
        ),
        scratch_shapes=scratch,
        compiler_params=pltpu.CompilerParams(vmem_limit_bytes=24 * 2**20),
    )(*args)


def core_groups(blk, grp):
    side = math.isqrt(blk // 2)

    def distance(chip):
        place, z = chip
        return sum(min(at, size - at) for at, size in ((place // side, side), (place % side, side), (z, grp)))

    chips = sorted(((place, z) for place in range(blk // 2) for z in range(grp)), key=lambda c: (distance(c), c))
    chips = chips[-1:] + chips[:-1]
    return [[(place * 2 + core) * grp + z for place, z in chips] for core in range(2)]


def per_device(rhs, diag_blocks, lower_blocks, upper_blocks, precond, coupling, send_cells, recv_cells, halo_len):
    fields, cells = rhs.shape
    peers = send_cells.shape[1]
    count = peers * lax.axis_size("grp") // 2
    vector = shape(8, cells)
    message = shape(peers * 8, LANES)
    args = (rhs, diag_blocks, lower_blocks, upper_blocks, precond, coupling, send_cells, recv_cells, halo_len)
    blocks = (diag_blocks, lower_blocks, upper_blocks)
    gram_shape = shape(2, 8, LANES)
    inputs = (precond, coupling, send_cells, halo_len, *blocks, recv_cells)
    u, z, msg, y, gram, *kept = call(
        first_kernel,
        (vector, vector, message, vector, gram_shape, *(jax.ShapeDtypeStruct(a.shape, a.dtype) for a in inputs)),
        rhs, *inputs,
        name="first",
        space=pltpu.HBM,
        scratch=(pltpu.VMEM(rhs.shape, jnp.float32), pltpu.SemaphoreType.DMA((2 * fields + 7,))),
    )
    face, blocks, recv_cells = kept[:4], kept[4:7], kept[7]
    us, zs, grams = [u], [z], [gram]
    for col in range(ITERS):
        got = lax.all_to_all(msg.reshape(peers, 8, LANES), "blk", 0, 0, tiled=True).reshape(peers * 8, LANES)
        if col < ITERS - 1:
            u, z, msg, y, gram = call(
                functools.partial(step_kernel, col + 1),
                (vector, vector, message, vector, gram_shape),
                got, recv_cells, y, *face, *blocks, *us,
                name="step",
            )
            zs.append(z)
            grams.append(gram)
        else:
            u, row = call(last_kernel, (vector, shape(8, LANES)), got, recv_cells, y, *us, *grams, name="last")
        us.append(u)
    other = lax.ppermute(row, "blk", [(i, i ^ 1) for i in range(peers)])
    (msg,) = call(pair_kernel, (shape(count, LANES),), row, other, name="pair")
    groups = core_groups(peers, lax.axis_size("grp"))
    got = lax.all_to_all(msg, BOTH, 0, 0, axis_index_groups=groups, tiled=True)
    adjoint, residual, flag = call(
        functools.partial(finish_kernel, count),
        (shape(fields, cells), shape(fields, cells), jax.ShapeDtypeStruct((1, LANES), jnp.int32)),
        got, *us, *zs,
        name="finish",
    )
    args, adjoint, residual, flag = lax.optimization_barrier((args, adjoint, residual, flag))
    return lax.switch(flag[0, 0], [lambda *_: arnoldi(*args), lambda *outs: outs], adjoint, residual)


def solution(mesh):
    return jax.shard_map(
        per_device,
        mesh=mesh,
        in_specs=(
            P(None, BOTH),
            P(None, None, BOTH),
            P(None, None, BOTH),
            P(None, None, BOTH),
            P(None, None, BOTH),
            P(BOTH, None, None, None, None),
            P(BOTH, None, None),
            P(BOTH, None, None),
            P(BOTH, None),
        ),
        out_specs=(P(None, BOTH), P(None, BOTH)),
        check_vma=False,
    )
```

```python
import functools
import math

import jax
import jax.numpy as jnp
from jax import lax
from jax.experimental import pallas as pl
from jax.experimental.pallas import tpu as pltpu
from jax.sharding import PartitionSpec as P

ITERS = 4
F = 7
LANES = 128
BOTH = ("blk", "grp")


def mixing(blocks, field):
    total = blocks[:, 0] * field[0][None]
    for inner in range(1, field.shape[0]):
        total = total + blocks[:, inner] * field[inner][None]
    return total


def operate(field, diag_blocks, lower_blocks, upper_blocks, masked, send_flat, recv_flat):
    fields = field.shape[0]
    peers, width = masked.shape[2:]
    zero_col = jnp.zeros((fields, 1), jnp.float32)
    before = jnp.concatenate([zero_col, field[:, :-1]], axis=1)
    after = jnp.concatenate([field[:, 1:], zero_col], axis=1)
    outgoing = jnp.take(field, send_flat, axis=1).reshape(fields, peers, width)
    term = lax.all_to_all(mixing(masked, outgoing), "blk", split_axis=1, concat_axis=1, tiled=True)
    local = mixing(diag_blocks, field) + mixing(lower_blocks, before) + mixing(upper_blocks, after)
    return local.at[:, recv_flat].add(term.reshape(fields, -1))


def arnoldi(rhs, diag_blocks, lower_blocks, upper_blocks, precond, coupling, send_cells, recv_cells, halo_len):
    slots = jnp.arange(coupling.shape[4], dtype=jnp.int32)
    live = (slots[None, :] < halo_len[0][:, None]).astype(jnp.float32)
    masked = coupling[0] * live[None, None, :, :]
    send_flat = send_cells[0].reshape(-1)
    recv_flat = recv_cells[0].reshape(-1)

    def apply_op(field):
        return operate(field, diag_blocks, lower_blocks, upper_blocks, masked, send_flat, recv_flat)

    beta = jnp.sqrt(lax.psum(jnp.sum(rhs * rhs), BOTH))
    basis = [rhs / beta]
    hess = jnp.zeros((ITERS + 1, ITERS), jnp.float32)
    for col in range(ITERS):
        product = apply_op(mixing(precond, basis[col]))
        proj = lax.psum(jnp.stack([jnp.sum(vector * product) for vector in basis]), BOTH)
        remain = product
        for index in range(col + 1):
            remain = remain - proj[index] * basis[index]
        height = jnp.sqrt(lax.psum(jnp.sum(remain * remain), BOTH))
        hess = hess.at[: col + 1, col].set(proj).at[col + 1, col].set(height)
        basis.append(remain / height)
    gram = jnp.dot(hess.T, hess, precision=lax.Precision.HIGHEST)
    factor = jnp.linalg.cholesky(gram)
    coef = jax.scipy.linalg.cho_solve((factor, True), beta * hess[0])
    combo = coef[0] * basis[0]
    for index in range(1, ITERS):
        combo = combo + coef[index] * basis[index]
    adjoint = mixing(precond, combo)
    return adjoint, rhs - apply_op(adjoint)


def two_sum(a, b):
    s = a + b
    t = s - a
    return s, (a - (s - t)) + (b - t)


def quick_sum(a, b):
    s = a + b
    return s, b - (s - a)


def halves(a):
    t = a * 4097.0
    high = t - (t - a)
    return high, a - high


def two_prod(a, ah, al, b, bh, bl):
    p = a * b
    return p, ((ah * bh - p) + ah * bl + al * bh) + al * bl


def dd_add(a, b):
    s, e = two_sum(a[0], b[0])
    return quick_sum(s, e + (a[1] + b[1]))


def dd_mul(a, b):
    p, e = two_prod(a[0], *halves(a[0]), b[0], *halves(b[0]))
    return quick_sum(p, e + (a[0] * b[1] + a[1] * b[0]))


def dd_neg(a):
    return -a[0], -a[1]


def dd_over(a, b, inverse):
    q = a[0] * inverse
    rest = dd_add(a, dd_neg(dd_mul(b, (q, jnp.zeros_like(q)))))
    return quick_sum(q, rest[0] * inverse)


def far_place(blk):
    side = math.isqrt(blk // 2)
    return (side // 2) * (side + 1) * 2


def row_sums(parts):
    rows = [jnp.sum(part, axis=0, keepdims=True) for part in parts]
    return jnp.concatenate(rows + [jnp.zeros_like(rows[0])], axis=0)


def precondition(pre_ref, u):
    return row_sums([pre_ref[i] * u[:F] for i in range(F)])


def gather(z, send_ref):
    cells = z.shape[1]
    tiles = cells // LANES
    source = [
        [jnp.broadcast_to(z[f : f + 1, t * LANES : (t + 1) * LANES], (8, LANES)) for t in range(tiles)]
        for f in range(F)
    ]
    taken = []
    for q in range(send_ref.shape[1] // 8):
        cell = send_ref[0, q * 8 : (q + 1) * 8, :]
        low = cell & (LANES - 1)
        high = cell >> 7
        taken.append([])
        for f in range(F):
            got = jnp.take_along_axis(source[f][0], low, axis=1, mode="promise_in_bounds")
            for t in range(1, tiles):
                other = jnp.take_along_axis(source[f][t], low, axis=1, mode="promise_in_bounds")
                got = jnp.where(high == t, other, got)
            taken[q].append(got)
    return taken


def mix(taken, coup_ref, halo_ref, msg_ref):
    peers = halo_ref.shape[1]
    lanes = lax.broadcasted_iota(jnp.int32, (8, LANES), 1)
    rows = lax.broadcasted_iota(jnp.int32, (8, peers), 0)
    cols = lax.broadcasted_iota(jnp.int32, (8, peers), 1)
    lens = jnp.broadcast_to(halo_ref[...], (8, peers))
    for q in range(peers // 8):
        size = jnp.sum(jnp.where(cols == rows + q * 8, lens, 0), axis=1, keepdims=True)
        live = lanes < size
        for i in range(F):
            total = coup_ref[0, i, 0, q * 8 : (q + 1) * 8, :] * taken[q][0]
            for j in range(1, F):
                total = total + coup_ref[0, i, j, q * 8 : (q + 1) * 8, :] * taken[q][j]
            total = jnp.where(live, total, 0.0)
            for half in (0, 4):
                place = (q * 8 + half) ^ far_place(peers)
                msg_ref[pl.ds(place * 8 + i, 4, stride=8), :] = total[half : half + 4]
        msg_ref[pl.ds(q * 64 + F, 8, stride=8), :] = jnp.zeros((8, LANES), jnp.float32)


def scatter(recv_ref, cells_ref, tiles):
    peers = cells_ref.shape[1]
    spots = lax.broadcasted_iota(jnp.int32, (LANES, LANES), 0)
    left, right = [], []
    for s in range(peers):
        x = recv_ref[s * 8 : (s + 1) * 8, :]
        first = x.astype(jnp.bfloat16).astype(jnp.float32)
        second = x - first
        source = s ^ far_place(peers)
        cell = cells_ref[0, source : source + 1, :]
        low = jnp.broadcast_to(cell & (LANES - 1), (LANES, LANES))
        high = jnp.broadcast_to(cell >> 7, (8, LANES))
        pieces = []
        for t in range(tiles):
            here = high == t
            pieces += [jnp.where(here, part, 0.0) for part in (first, second)]
        left.append(jnp.concatenate(pieces, axis=0).astype(jnp.bfloat16))
        right.append(jnp.where(spots == low, 1.0, 0.0).astype(jnp.bfloat16))
    total = lax.dot_general(
        jnp.concatenate(left, axis=1),
        jnp.concatenate(right, axis=1),
        (((1,), (1,)), ((), ())),
        preferred_element_type=jnp.float32,
    )
    out = []
    for t in range(tiles):
        out.append(total[t * 16 : t * 16 + 8] + total[t * 16 + 8 : t * 16 + 16])
    return jnp.concatenate(out, axis=1)


def local_part(z, diag_ref, low_ref, up_ref):
    cells = z.shape[1]
    col = lax.broadcasted_iota(jnp.int32, z.shape, 1)
    before = jnp.where(col == 0, 0.0, pltpu.roll(z, 1, 1))[:F]
    after = jnp.where(col == cells - 1, 0.0, pltpu.roll(z, cells - 1, 1))[:F]
    z = z[:F]
    return row_sums([diag_ref[i] * z + low_ref[i] * before + up_ref[i] * after for i in range(F)])


def products(us, last):
    cells = last.shape[1]
    tiles = [slice(t * LANES, (t + 1) * LANES) for t in range(cells // LANES)]
    lh, ll = halves(last)
    rows = lax.broadcasted_iota(jnp.int32, (8, LANES), 0)
    hi = jnp.zeros((8, LANES), jnp.float32)
    lo = jnp.zeros((8, LANES), jnp.float32)
    for i, u in enumerate(us):
        uh, ul = halves(u)
        terms = []
        for t in tiles:
            terms.append(two_prod(u[:, t], uh[:, t], ul[:, t], last[:, t], lh[:, t], ll[:, t]))
        while len(terms) > 1:
            terms = [dd_add(terms[k], terms[k + 1]) for k in range(0, len(terms), 2)]
        total = terms[0]
        for shift in (4, 2, 1):
            total = dd_add(total, tuple(pltpu.roll(v, shift, 0) for v in total))
        hi = jnp.where(rows == i, total[0], hi)
        lo = jnp.where(rows == i, total[1], lo)
    return hi, lo


def lane_sum(hi, lo):
    top = jnp.max(jnp.abs(hi), axis=1, keepdims=True) * 8192.0
    coarse = (hi + top) - top
    fine = (hi - coarse) + lo
    return quick_sum(jnp.sum(coarse, axis=1, keepdims=True), jnp.sum(fine, axis=1, keepdims=True))


def first_kernel(
    rhs_hbm, pre_hbm, coup_hbm, send_hbm, halo_hbm, diag_hbm, low_hbm, up_hbm, cells_hbm,
    u_ref, z_ref, msg_ref, y_ref, gram_ref, pre_ref, coup_ref, send_ref, halo_ref, diag_ref, low_ref, up_ref, cells_ref,
    rhs_ref, sems,
):
    whole = [(rhs_hbm, rhs_ref), (send_hbm, send_ref), (halo_hbm, halo_ref)]
    rows = [(pre_hbm, pre_ref)]
    faces = [(coup_hbm, coup_ref)]
    blocks = [(diag_hbm, diag_ref), (low_hbm, low_ref), (up_hbm, up_ref), (cells_hbm, cells_ref)]
    copies = [pltpu.make_async_copy(*pair, sems.at[k]) for k, pair in enumerate(whole + rows + faces + blocks)]
    for copy in copies:
        copy.start()
    for copy in copies[: len(whole)]:
        copy.wait()
    u = jnp.concatenate([rhs_ref[...], jnp.zeros((1, rhs_ref.shape[1]), jnp.float32)], axis=0)
    u_ref[...] = u
    gram_ref[0], gram_ref[1] = products([u], u)
    for copy in copies[len(whole) : len(whole) + 1]:
        copy.wait()
    z = precondition(pre_ref, u)
    z_ref[...] = z
    taken = gather(z, send_ref)
    for copy in copies[len(whole) + 1 : len(whole) + 2]:
        copy.wait()
    mix(taken, coup_ref, halo_ref, msg_ref)
    for copy in copies[len(whole) + 2 :]:
        copy.wait()
    y_ref[...] = local_part(z, diag_ref, low_ref, up_ref)


def step_kernel(col, recv_ref, cells_ref, y_ref, pre_ref, coup_ref, send_ref, halo_ref, diag_ref, low_ref, up_ref, *refs):
    u_refs, (u_ref, z_ref, msg_ref, next_ref, gram_ref) = refs[:col], refs[col:]
    u = y_ref[...] + scatter(recv_ref, cells_ref, y_ref.shape[1] // LANES)
    z = precondition(pre_ref, u)
    u_ref[...] = u
    z_ref[...] = z
    mix(gather(z, send_ref), coup_ref, halo_ref, msg_ref)
    next_ref[...] = local_part(z, diag_ref, low_ref, up_ref)
    gram_ref[0], gram_ref[1] = products([ref[...] for ref in u_refs] + [u], u)


def last_kernel(recv_ref, cells_ref, y_ref, *refs):
    u_refs, gram_refs, (u_ref, row_ref) = refs[:ITERS], refs[ITERS : 2 * ITERS], refs[2 * ITERS :]
    u = y_ref[...] + scatter(recv_ref, cells_ref, y_ref.shape[1] // LANES)
    u_ref[...] = u
    columns = [(ref[0], ref[1]) for ref in gram_refs]
    columns.append(products([ref[...] for ref in u_refs] + [u], u))
    lane = lax.broadcasted_iota(jnp.int32, (8, LANES), 1)
    row = lax.broadcasted_iota(jnp.int32, (8, LANES), 0)
    placed = jnp.zeros((8, LANES), jnp.float32)
    for j in range(ITERS + 1):
        for part, total in enumerate(lane_sum(*columns[j])):
            placed = jnp.where(lane == row + (part * 64 + 8 * j), total, placed)
    row_ref[...] = jnp.broadcast_to(jnp.sum(placed, axis=0, keepdims=True), row_ref.shape)


def pair_kernel(own_ref, other_ref, msg_ref):
    total, error = two_sum(own_ref[...], other_ref[...])
    lane = lax.broadcasted_iota(jnp.int32, total.shape, 1)
    row = jnp.where(lane < 64, total, total + pltpu.roll(error, 64, 1))
    msg_ref[...] = jnp.concatenate([row] * (msg_ref.shape[0] // 8), axis=0)


def finish_kernel(count, got_ref, *refs):
    u_refs, z_refs = refs[: ITERS + 1], refs[ITERS + 1 : 2 * ITERS + 1]
    adj_ref, res_ref, flag_ref = refs[2 * ITERS + 1 :]
    lane = lax.broadcasted_iota(jnp.int32, (8, LANES), 1)
    rows = [got_ref[8 * k : 8 * k + 8, :] for k in range(count // 8)]
    pairs = [two_sum(rows[k], rows[k + 1]) for k in range(0, len(rows), 2)]
    while len(pairs) > 1:
        pairs = [dd_add(pairs[k], pairs[k + 1]) for k in range(0, len(pairs), 2)]
    total = pairs[0]
    for shift in (4, 2, 1):
        total = dd_add(total, tuple(pltpu.roll(v, shift, 0) for v in total))
    total = dd_add(total, tuple(pltpu.roll(v, 64, 1) for v in total))

    def entry(i, j):
        i, j = min(i, j), max(i, j)
        at = 8 * j + i
        return tuple(jnp.broadcast_to(v[0:1, at : at + 1], (1, LANES)) for v in total)

    n = ITERS
    mat = [[entry(i + 1, j + 1) if j >= i else None for j in range(n)] for i in range(n)]
    vec = [entry(0, i + 1) for i in range(n)]
    norms = [mat[i][i][0] for i in range(n)]
    first = entry(0, 0)
    ok = (first[0] > 1e-20) & (first[0] < 1e30)
    left = first
    scaled = [None] * n
    factor = [[None] * n for _ in range(n)]
    for k in range(n):
        pivot = mat[k][k]
        ok = ok & (norms[k] > 1e-20) & (norms[k] < 1e30) & (pivot[0] > 1e-9 * norms[k])
        inverse = 1.0 / pivot[0]
        scaled[k] = dd_over(vec[k], pivot, inverse)
        left = dd_add(left, dd_neg(dd_mul(vec[k], scaled[k])))
        for j in range(k + 1, n):
            factor[k][j] = dd_over(mat[k][j], pivot, inverse)
        for i in range(k + 1, n):
            for j in range(i, n):
                mat[i][j] = dd_add(mat[i][j], dd_neg(dd_mul(factor[k][i], mat[k][j])))
            vec[i] = dd_add(vec[i], dd_neg(dd_mul(factor[k][i], vec[k])))
    coef = [None] * n
    for k in reversed(range(n)):
        value = scaled[k]
        for j in range(k + 1, n):
            value = dd_add(value, dd_neg(dd_mul(factor[k][j], coef[j])))
        coef[k] = value
    reach = jnp.zeros((1, LANES), jnp.float32)
    for k in range(n):
        reach = reach + jnp.abs(coef[k][0]) * jnp.sqrt(norms[k])
    ok = ok & (reach * reach < 1e7 * left[0])
    flag_ref[...] = jnp.where(ok, 1, 0)
    cells = adj_ref.shape[1]
    weight = [jnp.broadcast_to(coef[k][0][:, :1], (8, cells)) for k in range(n)]
    adj = weight[0] * z_refs[0][...]
    res = u_refs[0][...] - weight[0] * u_refs[1][...]
    for k in range(1, n):
        adj = adj + weight[k] * z_refs[k][...]
        res = res - weight[k] * u_refs[k + 1][...]
    adj_ref[...] = adj[:F]
    res_ref[...] = res[:F]


def shape(*dims):
    return jax.ShapeDtypeStruct(dims, jnp.float32)


def call(kernel, out, *args, name, space=pltpu.VMEM, scratch=()):
    return pl.pallas_call(
        kernel,
        out_shape=out,
        name=name,
        in_specs=[pl.BlockSpec(memory_space=space)] * len(args),
        out_specs=tuple(
            pl.BlockSpec(memory_space=pltpu.SMEM if o.shape == (1,) else pltpu.VMEM) for o in out
        ),
        scratch_shapes=scratch,
        compiler_params=pltpu.CompilerParams(vmem_limit_bytes=24 * 2**20),
    )(*args)


def core_groups(blk, grp):
    side = math.isqrt(blk // 2)

    def distance(chip):
        place, z = chip
        return sum(min(at, size - at) for at, size in ((place // side, side), (place % side, side), (z, grp)))

    chips = sorted(((place, z) for place in range(blk // 2) for z in range(grp)), key=lambda c: (distance(c), c))
    chips = chips[-1:] + chips[:-1]
    return [[(place * 2 + core) * grp + z for place, z in chips] for core in range(2)]


def per_device(rhs, diag_blocks, lower_blocks, upper_blocks, precond, coupling, send_cells, recv_cells, halo_len):
    fields, cells = rhs.shape
    peers = send_cells.shape[1]
    count = peers * lax.axis_size("grp") // 2
    vector = shape(8, cells)
    message = shape(peers * 8, LANES)
    args = (rhs, diag_blocks, lower_blocks, upper_blocks, precond, coupling, send_cells, recv_cells, halo_len)
    blocks = (diag_blocks, lower_blocks, upper_blocks)
    gram_shape = shape(2, 8, LANES)
    inputs = (precond, coupling, send_cells, halo_len, *blocks, recv_cells)
    u, z, msg, y, gram, *kept = call(
        first_kernel,
        (vector, vector, message, vector, gram_shape, *(jax.ShapeDtypeStruct(a.shape, a.dtype) for a in inputs)),
        rhs, *inputs,
        name="first",
        space=pltpu.HBM,
        scratch=(pltpu.VMEM(rhs.shape, jnp.float32), pltpu.SemaphoreType.DMA((2 * fields + 7,))),
    )
    face, blocks, recv_cells = kept[:4], kept[4:7], kept[7]
    us, zs, grams = [u], [z], [gram]
    order = [i ^ far_place(peers) for i in range(peers)]
    for col in range(ITERS):
        got = lax.all_to_all(msg.reshape(peers, 8, LANES), "blk", 0, 0, axis_index_groups=[order], tiled=True)
        got = got.reshape(peers * 8, LANES)
        if col < ITERS - 1:
            u, z, msg, y, gram = call(
                functools.partial(step_kernel, col + 1),
                (vector, vector, message, vector, gram_shape),
                got, recv_cells, y, *face, *blocks, *us,
                name="step",
            )
            zs.append(z)
            grams.append(gram)
        else:
            u, row = call(last_kernel, (vector, shape(8, LANES)), got, recv_cells, y, *us, *grams, name="last")
        us.append(u)
    other = lax.ppermute(row, "blk", [(i, i ^ 1) for i in range(peers)])
    (msg,) = call(pair_kernel, (shape(count, LANES),), row, other, name="pair")
    groups = core_groups(peers, lax.axis_size("grp"))
    got = lax.all_to_all(msg, BOTH, 0, 0, axis_index_groups=groups, tiled=True)
    adjoint, residual, flag = call(
        functools.partial(finish_kernel, count),
        (shape(fields, cells), shape(fields, cells), jax.ShapeDtypeStruct((1, LANES), jnp.int32)),
        got, *us, *zs,
        name="finish",
    )
    args, adjoint, residual, flag = lax.optimization_barrier((args, adjoint, residual, flag))
    return lax.switch(flag[0, 0], [lambda *_: arnoldi(*args), lambda *outs: outs], adjoint, residual)


def solution(mesh):
    return jax.shard_map(
        per_device,
        mesh=mesh,
        in_specs=(
            P(None, BOTH),
            P(None, None, BOTH),
            P(None, None, BOTH),
            P(None, None, BOTH),
            P(None, None, BOTH),
            P(BOTH, None, None, None, None),
            P(BOTH, None, None),
            P(BOTH, None, None),
            P(BOTH, None),
        ),
        out_specs=(P(None, BOTH), P(None, BOTH)),
        check_vma=False,
    )
```

```python
import functools
import math

import jax
import jax.numpy as jnp
from jax import lax
from jax.experimental import pallas as pl
from jax.experimental.pallas import tpu as pltpu
from jax.sharding import PartitionSpec as P

ITERS = 4
F = 7
LANES = 128
BOTH = ("blk", "grp")


def mixing(blocks, field):
    total = blocks[:, 0] * field[0][None]
    for inner in range(1, field.shape[0]):
        total = total + blocks[:, inner] * field[inner][None]
    return total


def operate(field, diag_blocks, lower_blocks, upper_blocks, masked, send_flat, recv_flat):
    fields = field.shape[0]
    peers, width = masked.shape[2:]
    zero_col = jnp.zeros((fields, 1), jnp.float32)
    before = jnp.concatenate([zero_col, field[:, :-1]], axis=1)
    after = jnp.concatenate([field[:, 1:], zero_col], axis=1)
    outgoing = jnp.take(field, send_flat, axis=1).reshape(fields, peers, width)
    term = lax.all_to_all(mixing(masked, outgoing), "blk", split_axis=1, concat_axis=1, tiled=True)
    local = mixing(diag_blocks, field) + mixing(lower_blocks, before) + mixing(upper_blocks, after)
    return local.at[:, recv_flat].add(term.reshape(fields, -1))


def arnoldi(rhs, diag_blocks, lower_blocks, upper_blocks, precond, coupling, send_cells, recv_cells, halo_len):
    slots = jnp.arange(coupling.shape[4], dtype=jnp.int32)
    live = (slots[None, :] < halo_len[0][:, None]).astype(jnp.float32)
    masked = coupling[0] * live[None, None, :, :]
    send_flat = send_cells[0].reshape(-1)
    recv_flat = recv_cells[0].reshape(-1)

    def apply_op(field):
        return operate(field, diag_blocks, lower_blocks, upper_blocks, masked, send_flat, recv_flat)

    beta = jnp.sqrt(lax.psum(jnp.sum(rhs * rhs), BOTH))
    basis = [rhs / beta]
    hess = jnp.zeros((ITERS + 1, ITERS), jnp.float32)
    for col in range(ITERS):
        product = apply_op(mixing(precond, basis[col]))
        proj = lax.psum(jnp.stack([jnp.sum(vector * product) for vector in basis]), BOTH)
        remain = product
        for index in range(col + 1):
            remain = remain - proj[index] * basis[index]
        height = jnp.sqrt(lax.psum(jnp.sum(remain * remain), BOTH))
        hess = hess.at[: col + 1, col].set(proj).at[col + 1, col].set(height)
        basis.append(remain / height)
    gram = jnp.dot(hess.T, hess, precision=lax.Precision.HIGHEST)
    factor = jnp.linalg.cholesky(gram)
    coef = jax.scipy.linalg.cho_solve((factor, True), beta * hess[0])
    combo = coef[0] * basis[0]
    for index in range(1, ITERS):
        combo = combo + coef[index] * basis[index]
    adjoint = mixing(precond, combo)
    return adjoint, rhs - apply_op(adjoint)


def two_sum(a, b):
    s = a + b
    t = s - a
    return s, (a - (s - t)) + (b - t)


def quick_sum(a, b):
    s = a + b
    return s, b - (s - a)


def halves(a):
    t = a * 4097.0
    high = t - (t - a)
    return high, a - high


def two_prod(a, ah, al, b, bh, bl):
    p = a * b
    return p, ((ah * bh - p) + ah * bl + al * bh) + al * bl


def dd_add(a, b):
    s, e = two_sum(a[0], b[0])
    return quick_sum(s, e + (a[1] + b[1]))


def dd_mul(a, b):
    p, e = two_prod(a[0], *halves(a[0]), b[0], *halves(b[0]))
    return quick_sum(p, e + (a[0] * b[1] + a[1] * b[0]))


def dd_neg(a):
    return -a[0], -a[1]


def dd_over(a, b, inverse):
    q = a[0] * inverse
    rest = dd_add(a, dd_neg(dd_mul(b, (q, jnp.zeros_like(q)))))
    return quick_sum(q, rest[0] * inverse)


def far_place(blk):
    side = math.isqrt(blk // 2)
    return (side // 2) * (side + 1) * 2 + 1


def flip(value, bits):
    half, bit = bits & 4, bits & 3
    if bit == 0:
        return pltpu.roll(value, half, 0) if half else value
    rows = lax.broadcasted_iota(jnp.int32, value.shape, 0)
    return jnp.where((rows & bit) == 0, pltpu.roll(value, 8 - bit - half, 0), pltpu.roll(value, bit + half, 0))


def row_sums(parts):
    rows = [jnp.sum(part, axis=0, keepdims=True) for part in parts]
    return jnp.concatenate(rows + [jnp.zeros_like(rows[0])], axis=0)


def precondition(pre_ref, u):
    return row_sums([pre_ref[i] * u[:F] for i in range(F)])


def gather(z, send_ref):
    cells = z.shape[1]
    tiles = cells // LANES
    source = [
        [jnp.broadcast_to(z[f : f + 1, t * LANES : (t + 1) * LANES], (8, LANES)) for t in range(tiles)]
        for f in range(F)
    ]
    taken = []
    for q in range(send_ref.shape[1] // 8):
        cell = send_ref[0, q * 8 : (q + 1) * 8, :]
        low = cell & (LANES - 1)
        high = cell >> 7
        taken.append([])
        for f in range(F):
            got = jnp.take_along_axis(source[f][0], low, axis=1, mode="promise_in_bounds")
            for t in range(1, tiles):
                other = jnp.take_along_axis(source[f][t], low, axis=1, mode="promise_in_bounds")
                got = jnp.where(high == t, other, got)
            taken[q].append(got)
    return taken


def mix(taken, coup_ref, halo_ref, msg_ref):
    peers = halo_ref.shape[1]
    far = far_place(peers)
    lanes = lax.broadcasted_iota(jnp.int32, (8, LANES), 1)
    rows = lax.broadcasted_iota(jnp.int32, (8, peers), 0)
    cols = lax.broadcasted_iota(jnp.int32, (8, peers), 1)
    lens = jnp.broadcast_to(halo_ref[...], (8, peers))
    for q in range(peers // 8):
        size = jnp.sum(jnp.where(cols == rows + q * 8, lens, 0), axis=1, keepdims=True)
        live = lanes < size
        place = (q * 8) ^ (far & ~7)
        for i in range(F):
            total = coup_ref[0, i, 0, q * 8 : (q + 1) * 8, :] * taken[q][0]
            for j in range(1, F):
                total = total + coup_ref[0, i, j, q * 8 : (q + 1) * 8, :] * taken[q][j]
            msg_ref[pl.ds(place * 8 + i, 8, stride=8), :] = flip(jnp.where(live, total, 0.0), far & 7)
        msg_ref[pl.ds(q * 64 + F, 8, stride=8), :] = jnp.zeros((8, LANES), jnp.float32)


def scatter(recv_ref, cells_ref, tiles):
    peers = cells_ref.shape[1]
    spots = lax.broadcasted_iota(jnp.int32, (LANES, LANES), 0)
    left, right = [], []
    for s in range(peers):
        x = recv_ref[s * 8 : (s + 1) * 8, :]
        first = x.astype(jnp.bfloat16).astype(jnp.float32)
        second = x - first
        source = s ^ far_place(peers)
        cell = cells_ref[0, source : source + 1, :]
        low = jnp.broadcast_to(cell & (LANES - 1), (LANES, LANES))
        high = jnp.broadcast_to(cell >> 7, (8, LANES))
        pieces = []
        for t in range(tiles):
            here = high == t
            pieces += [jnp.where(here, part, 0.0) for part in (first, second)]
        left.append(jnp.concatenate(pieces, axis=0).astype(jnp.bfloat16))
        right.append(jnp.where(spots == low, 1.0, 0.0).astype(jnp.bfloat16))
    total = lax.dot_general(
        jnp.concatenate(left, axis=1),
        jnp.concatenate(right, axis=1),
        (((1,), (1,)), ((), ())),
        preferred_element_type=jnp.float32,
    )
    out = []
    for t in range(tiles):
        out.append(total[t * 16 : t * 16 + 8] + total[t * 16 + 8 : t * 16 + 16])
    return jnp.concatenate(out, axis=1)


def local_part(z, diag_ref, low_ref, up_ref):
    cells = z.shape[1]
    col = lax.broadcasted_iota(jnp.int32, z.shape, 1)
    before = jnp.where(col == 0, 0.0, pltpu.roll(z, 1, 1))[:F]
    after = jnp.where(col == cells - 1, 0.0, pltpu.roll(z, cells - 1, 1))[:F]
    z = z[:F]
    return row_sums([diag_ref[i] * z + low_ref[i] * before + up_ref[i] * after for i in range(F)])


def products(us, last):
    cells = last.shape[1]
    tiles = [slice(t * LANES, (t + 1) * LANES) for t in range(cells // LANES)]
    lh, ll = halves(last)
    rows = lax.broadcasted_iota(jnp.int32, (8, LANES), 0)
    hi = jnp.zeros((8, LANES), jnp.float32)
    lo = jnp.zeros((8, LANES), jnp.float32)
    for i, u in enumerate(us):
        uh, ul = halves(u)
        terms = []
        for t in tiles:
            terms.append(two_prod(u[:, t], uh[:, t], ul[:, t], last[:, t], lh[:, t], ll[:, t]))
        while len(terms) > 1:
            terms = [dd_add(terms[k], terms[k + 1]) for k in range(0, len(terms), 2)]
        total = terms[0]
        for shift in (4, 2, 1):
            total = dd_add(total, tuple(pltpu.roll(v, shift, 0) for v in total))
        hi = jnp.where(rows == i, total[0], hi)
        lo = jnp.where(rows == i, total[1], lo)
    return hi, lo


def lane_sum(hi, lo):
    top = jnp.max(jnp.abs(hi), axis=1, keepdims=True) * 8192.0
    coarse = (hi + top) - top
    fine = (hi - coarse) + lo
    return quick_sum(jnp.sum(coarse, axis=1, keepdims=True), jnp.sum(fine, axis=1, keepdims=True))


def first_kernel(
    rhs_hbm, pre_hbm, coup_hbm, send_hbm, halo_hbm, diag_hbm, low_hbm, up_hbm, cells_hbm,
    u_ref, z_ref, msg_ref, y_ref, gram_ref, pre_ref, coup_ref, send_ref, halo_ref, diag_ref, low_ref, up_ref, cells_ref,
    rhs_ref, sems,
):
    whole = [(rhs_hbm, rhs_ref), (send_hbm, send_ref), (halo_hbm, halo_ref)]
    rows = [(pre_hbm, pre_ref)]
    faces = [(coup_hbm, coup_ref)]
    blocks = [(diag_hbm, diag_ref), (low_hbm, low_ref), (up_hbm, up_ref), (cells_hbm, cells_ref)]
    copies = [pltpu.make_async_copy(*pair, sems.at[k]) for k, pair in enumerate(whole + rows + faces + blocks)]
    for copy in copies:
        copy.start()
    for copy in copies[: len(whole)]:
        copy.wait()
    u = jnp.concatenate([rhs_ref[...], jnp.zeros((1, rhs_ref.shape[1]), jnp.float32)], axis=0)
    u_ref[...] = u
    gram_ref[0], gram_ref[1] = products([u], u)
    for copy in copies[len(whole) : len(whole) + 1]:
        copy.wait()
    z = precondition(pre_ref, u)
    z_ref[...] = z
    taken = gather(z, send_ref)
    for copy in copies[len(whole) + 1 : len(whole) + 2]:
        copy.wait()
    mix(taken, coup_ref, halo_ref, msg_ref)
    for copy in copies[len(whole) + 2 :]:
        copy.wait()
    y_ref[...] = local_part(z, diag_ref, low_ref, up_ref)


def step_kernel(col, recv_ref, cells_ref, y_ref, pre_ref, coup_ref, send_ref, halo_ref, diag_ref, low_ref, up_ref, *refs):
    u_refs, (u_ref, z_ref, msg_ref, next_ref, gram_ref) = refs[:col], refs[col:]
    u = y_ref[...] + scatter(recv_ref, cells_ref, y_ref.shape[1] // LANES)
    z = precondition(pre_ref, u)
    u_ref[...] = u
    z_ref[...] = z
    mix(gather(z, send_ref), coup_ref, halo_ref, msg_ref)
    next_ref[...] = local_part(z, diag_ref, low_ref, up_ref)
    gram_ref[0], gram_ref[1] = products([ref[...] for ref in u_refs] + [u], u)


def last_kernel(recv_ref, cells_ref, y_ref, *refs):
    u_refs, gram_refs, (u_ref, row_ref) = refs[:ITERS], refs[ITERS : 2 * ITERS], refs[2 * ITERS :]
    u = y_ref[...] + scatter(recv_ref, cells_ref, y_ref.shape[1] // LANES)
    u_ref[...] = u
    columns = [(ref[0], ref[1]) for ref in gram_refs]
    columns.append(products([ref[...] for ref in u_refs] + [u], u))
    lane = lax.broadcasted_iota(jnp.int32, (8, LANES), 1)
    row = lax.broadcasted_iota(jnp.int32, (8, LANES), 0)
    placed = jnp.zeros((8, LANES), jnp.float32)
    for j in range(ITERS + 1):
        for part, total in enumerate(lane_sum(*columns[j])):
            placed = jnp.where(lane == row + (part * 64 + 8 * j), total, placed)
    row_ref[...] = jnp.broadcast_to(jnp.sum(placed, axis=0, keepdims=True), row_ref.shape)


def pair_kernel(own_ref, other_ref, msg_ref):
    total, error = two_sum(own_ref[...], other_ref[...])
    lane = lax.broadcasted_iota(jnp.int32, total.shape, 1)
    row = jnp.where(lane < 64, total, total + pltpu.roll(error, 64, 1))
    msg_ref[...] = jnp.concatenate([row] * (msg_ref.shape[0] // 8), axis=0)


def finish_kernel(count, got_ref, *refs):
    u_refs, z_refs = refs[: ITERS + 1], refs[ITERS + 1 : 2 * ITERS + 1]
    adj_ref, res_ref, flag_ref = refs[2 * ITERS + 1 :]
    lane = lax.broadcasted_iota(jnp.int32, (8, LANES), 1)
    rows = [got_ref[8 * k : 8 * k + 8, :] for k in range(count // 8)]
    pairs = [two_sum(rows[k], rows[k + 1]) for k in range(0, len(rows), 2)]
    while len(pairs) > 1:
        pairs = [dd_add(pairs[k], pairs[k + 1]) for k in range(0, len(pairs), 2)]
    total = pairs[0]
    for shift in (4, 2, 1):
        total = dd_add(total, tuple(pltpu.roll(v, shift, 0) for v in total))
    total = dd_add(total, tuple(pltpu.roll(v, 64, 1) for v in total))

    def entry(i, j):
        i, j = min(i, j), max(i, j)
        at = 8 * j + i
        return tuple(jnp.broadcast_to(v[0:1, at : at + 1], (1, LANES)) for v in total)

    n = ITERS
    mat = [[entry(i + 1, j + 1) if j >= i else None for j in range(n)] for i in range(n)]
    vec = [entry(0, i + 1) for i in range(n)]
    norms = [mat[i][i][0] for i in range(n)]
    first = entry(0, 0)
    ok = (first[0] > 1e-20) & (first[0] < 1e30)
    left = first
    scaled = [None] * n
    factor = [[None] * n for _ in range(n)]
    for k in range(n):
        pivot = mat[k][k]
        ok = ok & (norms[k] > 1e-20) & (norms[k] < 1e30) & (pivot[0] > 1e-9 * norms[k])
        inverse = 1.0 / pivot[0]
        scaled[k] = dd_over(vec[k], pivot, inverse)
        left = dd_add(left, dd_neg(dd_mul(vec[k], scaled[k])))
        for j in range(k + 1, n):
            factor[k][j] = dd_over(mat[k][j], pivot, inverse)
        for i in range(k + 1, n):
            for j in range(i, n):
                mat[i][j] = dd_add(mat[i][j], dd_neg(dd_mul(factor[k][i], mat[k][j])))
            vec[i] = dd_add(vec[i], dd_neg(dd_mul(factor[k][i], vec[k])))
    coef = [None] * n
    for k in reversed(range(n)):
        value = scaled[k]
        for j in range(k + 1, n):
            value = dd_add(value, dd_neg(dd_mul(factor[k][j], coef[j])))
        coef[k] = value
    reach = jnp.zeros((1, LANES), jnp.float32)
    for k in range(n):
        reach = reach + jnp.abs(coef[k][0]) * jnp.sqrt(norms[k])
    ok = ok & (reach * reach < 1e7 * left[0])
    flag_ref[...] = jnp.where(ok, 1, 0)
    cells = adj_ref.shape[1]
    weight = [jnp.broadcast_to(coef[k][0][:, :1], (8, cells)) for k in range(n)]
    adj = weight[0] * z_refs[0][...]
    res = u_refs[0][...] - weight[0] * u_refs[1][...]
    for k in range(1, n):
        adj = adj + weight[k] * z_refs[k][...]
        res = res - weight[k] * u_refs[k + 1][...]
    adj_ref[...] = adj[:F]
    res_ref[...] = res[:F]


def shape(*dims):
    return jax.ShapeDtypeStruct(dims, jnp.float32)


def call(kernel, out, *args, name, space=pltpu.VMEM, scratch=()):
    return pl.pallas_call(
        kernel,
        out_shape=out,
        name=name,
        in_specs=[pl.BlockSpec(memory_space=space)] * len(args),
        out_specs=tuple(
            pl.BlockSpec(memory_space=pltpu.SMEM if o.shape == (1,) else pltpu.VMEM) for o in out
        ),
        scratch_shapes=scratch,
        compiler_params=pltpu.CompilerParams(vmem_limit_bytes=24 * 2**20),
    )(*args)


def core_groups(blk, grp):
    side = math.isqrt(blk // 2)

    def distance(chip):
        place, z = chip
        return sum(min(at, size - at) for at, size in ((place // side, side), (place % side, side), (z, grp)))

    chips = sorted(((place, z) for place in range(blk // 2) for z in range(grp)), key=lambda c: (distance(c), c))
    chips = chips[-1:] + chips[:-1]
    return [[(place * 2 + core) * grp + z for place, z in chips] for core in range(2)]


def per_device(rhs, diag_blocks, lower_blocks, upper_blocks, precond, coupling, send_cells, recv_cells, halo_len):
    fields, cells = rhs.shape
    peers = send_cells.shape[1]
    count = peers * lax.axis_size("grp") // 2
    vector = shape(8, cells)
    message = shape(peers * 8, LANES)
    args = (rhs, diag_blocks, lower_blocks, upper_blocks, precond, coupling, send_cells, recv_cells, halo_len)
    blocks = (diag_blocks, lower_blocks, upper_blocks)
    gram_shape = shape(2, 8, LANES)
    inputs = (precond, coupling, send_cells, halo_len, *blocks, recv_cells)
    u, z, msg, y, gram, *kept = call(
        first_kernel,
        (vector, vector, message, vector, gram_shape, *(jax.ShapeDtypeStruct(a.shape, a.dtype) for a in inputs)),
        rhs, *inputs,
        name="first",
        space=pltpu.HBM,
        scratch=(pltpu.VMEM(rhs.shape, jnp.float32), pltpu.SemaphoreType.DMA((2 * fields + 7,))),
    )
    face, blocks, recv_cells = kept[:4], kept[4:7], kept[7]
    us, zs, grams = [u], [z], [gram]
    order = [i ^ far_place(peers) for i in range(peers)]
    for col in range(ITERS):
        got = lax.all_to_all(msg.reshape(peers, 8, LANES), "blk", 0, 0, axis_index_groups=[order], tiled=True)
        got = got.reshape(peers * 8, LANES)
        if col < ITERS - 1:
            u, z, msg, y, gram = call(
                functools.partial(step_kernel, col + 1),
                (vector, vector, message, vector, gram_shape),
                got, recv_cells, y, *face, *blocks, *us,
                name="step",
            )
            zs.append(z)
            grams.append(gram)
        else:
            u, row = call(last_kernel, (vector, shape(8, LANES)), got, recv_cells, y, *us, *grams, name="last")
        us.append(u)
    other = lax.ppermute(row, "blk", [(i, i ^ 1) for i in range(peers)])
    (msg,) = call(pair_kernel, (shape(count, LANES),), row, other, name="pair")
    groups = core_groups(peers, lax.axis_size("grp"))
    got = lax.all_to_all(msg, BOTH, 0, 0, axis_index_groups=groups, tiled=True)
    adjoint, residual, flag = call(
        functools.partial(finish_kernel, count),
        (shape(fields, cells), shape(fields, cells), jax.ShapeDtypeStruct((1, LANES), jnp.int32)),
        got, *us, *zs,
        name="finish",
    )
    args, adjoint, residual, flag = lax.optimization_barrier((args, adjoint, residual, flag))
    return lax.switch(flag[0, 0], [lambda *_: arnoldi(*args), lambda *outs: outs], adjoint, residual)


def solution(mesh):
    return jax.shard_map(
        per_device,
        mesh=mesh,
        in_specs=(
            P(None, BOTH),
            P(None, None, BOTH),
            P(None, None, BOTH),
            P(None, None, BOTH),
            P(None, None, BOTH),
            P(BOTH, None, None, None, None),
            P(BOTH, None, None),
            P(BOTH, None, None),
            P(BOTH, None),
        ),
        out_specs=(P(None, BOTH), P(None, BOTH)),
        check_vma=False,
    )
```

```python
import functools
import math

import jax
import jax.numpy as jnp
from jax import lax
from jax.experimental import pallas as pl
from jax.experimental.pallas import tpu as pltpu
from jax.sharding import PartitionSpec as P

ITERS = 4
F = 7
LANES = 128
BOTH = ("blk", "grp")


def mixing(blocks, field):
    total = blocks[:, 0] * field[0][None]
    for inner in range(1, field.shape[0]):
        total = total + blocks[:, inner] * field[inner][None]
    return total


def operate(field, diag_blocks, lower_blocks, upper_blocks, masked, send_flat, recv_flat):
    fields = field.shape[0]
    peers, width = masked.shape[2:]
    zero_col = jnp.zeros((fields, 1), jnp.float32)
    before = jnp.concatenate([zero_col, field[:, :-1]], axis=1)
    after = jnp.concatenate([field[:, 1:], zero_col], axis=1)
    outgoing = jnp.take(field, send_flat, axis=1).reshape(fields, peers, width)
    term = lax.all_to_all(mixing(masked, outgoing), "blk", split_axis=1, concat_axis=1, tiled=True)
    local = mixing(diag_blocks, field) + mixing(lower_blocks, before) + mixing(upper_blocks, after)
    return local.at[:, recv_flat].add(term.reshape(fields, -1))


def arnoldi(rhs, diag_blocks, lower_blocks, upper_blocks, precond, coupling, send_cells, recv_cells, halo_len):
    slots = jnp.arange(coupling.shape[4], dtype=jnp.int32)
    live = (slots[None, :] < halo_len[0][:, None]).astype(jnp.float32)
    masked = coupling[0] * live[None, None, :, :]
    send_flat = send_cells[0].reshape(-1)
    recv_flat = recv_cells[0].reshape(-1)

    def apply_op(field):
        return operate(field, diag_blocks, lower_blocks, upper_blocks, masked, send_flat, recv_flat)

    beta = jnp.sqrt(lax.psum(jnp.sum(rhs * rhs), BOTH))
    basis = [rhs / beta]
    hess = jnp.zeros((ITERS + 1, ITERS), jnp.float32)
    for col in range(ITERS):
        product = apply_op(mixing(precond, basis[col]))
        proj = lax.psum(jnp.stack([jnp.sum(vector * product) for vector in basis]), BOTH)
        remain = product
        for index in range(col + 1):
            remain = remain - proj[index] * basis[index]
        height = jnp.sqrt(lax.psum(jnp.sum(remain * remain), BOTH))
        hess = hess.at[: col + 1, col].set(proj).at[col + 1, col].set(height)
        basis.append(remain / height)
    gram = jnp.dot(hess.T, hess, precision=lax.Precision.HIGHEST)
    factor = jnp.linalg.cholesky(gram)
    coef = jax.scipy.linalg.cho_solve((factor, True), beta * hess[0])
    combo = coef[0] * basis[0]
    for index in range(1, ITERS):
        combo = combo + coef[index] * basis[index]
    adjoint = mixing(precond, combo)
    return adjoint, rhs - apply_op(adjoint)


def two_sum(a, b):
    s = a + b
    t = s - a
    return s, (a - (s - t)) + (b - t)


def quick_sum(a, b):
    s = a + b
    return s, b - (s - a)


def halves(a):
    t = a * 4097.0
    high = t - (t - a)
    return high, a - high


def two_prod(a, ah, al, b, bh, bl):
    p = a * b
    return p, ((ah * bh - p) + ah * bl + al * bh) + al * bl


def dd_add(a, b):
    s, e = two_sum(a[0], b[0])
    return quick_sum(s, e + (a[1] + b[1]))


def dd_mul(a, b):
    p, e = two_prod(a[0], *halves(a[0]), b[0], *halves(b[0]))
    return quick_sum(p, e + (a[0] * b[1] + a[1] * b[0]))


def dd_neg(a):
    return -a[0], -a[1]


def dd_over(a, b, inverse):
    q = a[0] * inverse
    rest = dd_add(a, dd_neg(dd_mul(b, (q, jnp.zeros_like(q)))))
    return quick_sum(q, rest[0] * inverse)


def turns(blk):
    side = math.isqrt(blk // 2)
    return side // 2, side // 2 * 2 + 1


def place_of(peer, blk):
    y, turn = turns(blk)
    return (y - peer // 8) % (blk // 8) * 8 + (peer - turn) % 8


def row_sums(parts):
    rows = [jnp.sum(part, axis=0, keepdims=True) for part in parts]
    return jnp.concatenate(rows + [jnp.zeros_like(rows[0])], axis=0)


def precondition(pre_ref, u):
    return row_sums([pre_ref[i] * u[:F] for i in range(F)])


def gather(z, send_ref):
    cells = z.shape[1]
    tiles = cells // LANES
    source = [
        [jnp.broadcast_to(z[f : f + 1, t * LANES : (t + 1) * LANES], (8, LANES)) for t in range(tiles)]
        for f in range(F)
    ]
    taken = []
    for q in range(send_ref.shape[1] // 8):
        cell = send_ref[0, q * 8 : (q + 1) * 8, :]
        low = cell & (LANES - 1)
        high = cell >> 7
        taken.append([])
        for f in range(F):
            got = jnp.take_along_axis(source[f][0], low, axis=1, mode="promise_in_bounds")
            for t in range(1, tiles):
                other = jnp.take_along_axis(source[f][t], low, axis=1, mode="promise_in_bounds")
                got = jnp.where(high == t, other, got)
            taken[q].append(got)
    return taken


def mix(taken, coup_ref, halo_ref, msg_ref):
    peers = halo_ref.shape[1]
    turn = turns(peers)[1]
    lanes = lax.broadcasted_iota(jnp.int32, (8, LANES), 1)
    rows = lax.broadcasted_iota(jnp.int32, (8, peers), 0)
    cols = lax.broadcasted_iota(jnp.int32, (8, peers), 1)
    lens = jnp.broadcast_to(halo_ref[...], (8, peers))
    for q in range(peers // 8):
        size = jnp.sum(jnp.where(cols == rows + q * 8, lens, 0), axis=1, keepdims=True)
        live = lanes < size
        place = place_of(q * 8, peers) // 8 * 8
        for i in range(F):
            total = coup_ref[0, i, 0, q * 8 : (q + 1) * 8, :] * taken[q][0]
            for j in range(1, F):
                total = total + coup_ref[0, i, j, q * 8 : (q + 1) * 8, :] * taken[q][j]
            msg_ref[pl.ds(place * 8 + i, 8, stride=8), :] = pltpu.roll(jnp.where(live, total, 0.0), 8 - turn, 0)
        msg_ref[pl.ds(q * 64 + F, 8, stride=8), :] = jnp.zeros((8, LANES), jnp.float32)


def scatter(recv_ref, cells_ref, tiles):
    peers = cells_ref.shape[1]
    spots = lax.broadcasted_iota(jnp.int32, (LANES, LANES), 0)
    left, right = [], []
    for s in range(peers):
        place = place_of(s, peers)
        x = recv_ref[place * 8 : (place + 1) * 8, :]
        first = x.astype(jnp.bfloat16).astype(jnp.float32)
        second = x - first
        cell = cells_ref[0, s : s + 1, :]
        low = jnp.broadcast_to(cell & (LANES - 1), (LANES, LANES))
        high = jnp.broadcast_to(cell >> 7, (8, LANES))
        pieces = []
        for t in range(tiles):
            here = high == t
            pieces += [jnp.where(here, part, 0.0) for part in (first, second)]
        left.append(jnp.concatenate(pieces, axis=0).astype(jnp.bfloat16))
        right.append(jnp.where(spots == low, 1.0, 0.0).astype(jnp.bfloat16))
    total = lax.dot_general(
        jnp.concatenate(left, axis=1),
        jnp.concatenate(right, axis=1),
        (((1,), (1,)), ((), ())),
        preferred_element_type=jnp.float32,
    )
    out = []
    for t in range(tiles):
        out.append(total[t * 16 : t * 16 + 8] + total[t * 16 + 8 : t * 16 + 16])
    return jnp.concatenate(out, axis=1)


def local_part(z, diag_ref, low_ref, up_ref):
    cells = z.shape[1]
    col = lax.broadcasted_iota(jnp.int32, z.shape, 1)
    before = jnp.where(col == 0, 0.0, pltpu.roll(z, 1, 1))[:F]
    after = jnp.where(col == cells - 1, 0.0, pltpu.roll(z, cells - 1, 1))[:F]
    z = z[:F]
    return row_sums([diag_ref[i] * z + low_ref[i] * before + up_ref[i] * after for i in range(F)])


def products(us, last):
    cells = last.shape[1]
    tiles = [slice(t * LANES, (t + 1) * LANES) for t in range(cells // LANES)]
    lh, ll = halves(last)
    rows = lax.broadcasted_iota(jnp.int32, (8, LANES), 0)
    hi = jnp.zeros((8, LANES), jnp.float32)
    lo = jnp.zeros((8, LANES), jnp.float32)
    for i, u in enumerate(us):
        uh, ul = halves(u)
        terms = []
        for t in tiles:
            terms.append(two_prod(u[:, t], uh[:, t], ul[:, t], last[:, t], lh[:, t], ll[:, t]))
        while len(terms) > 1:
            terms = [dd_add(terms[k], terms[k + 1]) for k in range(0, len(terms), 2)]
        total = terms[0]
        for shift in (4, 2, 1):
            total = dd_add(total, tuple(pltpu.roll(v, shift, 0) for v in total))
        hi = jnp.where(rows == i, total[0], hi)
        lo = jnp.where(rows == i, total[1], lo)
    return hi, lo


def lane_sum(hi, lo):
    top = jnp.max(jnp.abs(hi), axis=1, keepdims=True) * 8192.0
    coarse = (hi + top) - top
    fine = (hi - coarse) + lo
    return quick_sum(jnp.sum(coarse, axis=1, keepdims=True), jnp.sum(fine, axis=1, keepdims=True))


def first_kernel(
    rhs_hbm, pre_hbm, coup_hbm, send_hbm, halo_hbm, diag_hbm, low_hbm, up_hbm, cells_hbm,
    u_ref, z_ref, msg_ref, y_ref, gram_ref, pre_ref, coup_ref, send_ref, halo_ref, diag_ref, low_ref, up_ref, cells_ref,
    rhs_ref, sems,
):
    whole = [(rhs_hbm, rhs_ref), (send_hbm, send_ref), (halo_hbm, halo_ref)]
    rows = [(pre_hbm, pre_ref)]
    faces = [(coup_hbm, coup_ref)]
    blocks = [(diag_hbm, diag_ref), (low_hbm, low_ref), (up_hbm, up_ref), (cells_hbm, cells_ref)]
    copies = [pltpu.make_async_copy(*pair, sems.at[k]) for k, pair in enumerate(whole + rows + faces + blocks)]
    for copy in copies:
        copy.start()
    for copy in copies[: len(whole)]:
        copy.wait()
    u = jnp.concatenate([rhs_ref[...], jnp.zeros((1, rhs_ref.shape[1]), jnp.float32)], axis=0)
    u_ref[...] = u
    gram_ref[0], gram_ref[1] = products([u], u)
    for copy in copies[len(whole) : len(whole) + 1]:
        copy.wait()
    z = precondition(pre_ref, u)
    z_ref[...] = z
    taken = gather(z, send_ref)
    for copy in copies[len(whole) + 1 : len(whole) + 2]:
        copy.wait()
    mix(taken, coup_ref, halo_ref, msg_ref)
    for copy in copies[len(whole) + 2 :]:
        copy.wait()
    y_ref[...] = local_part(z, diag_ref, low_ref, up_ref)


def step_kernel(col, recv_ref, cells_ref, y_ref, pre_ref, coup_ref, send_ref, halo_ref, diag_ref, low_ref, up_ref, *refs):
    u_refs, (u_ref, z_ref, msg_ref, next_ref, gram_ref) = refs[:col], refs[col:]
    u = y_ref[...] + scatter(recv_ref, cells_ref, y_ref.shape[1] // LANES)
    z = precondition(pre_ref, u)
    u_ref[...] = u
    z_ref[...] = z
    mix(gather(z, send_ref), coup_ref, halo_ref, msg_ref)
    next_ref[...] = local_part(z, diag_ref, low_ref, up_ref)
    gram_ref[0], gram_ref[1] = products([ref[...] for ref in u_refs] + [u], u)


def last_kernel(recv_ref, cells_ref, y_ref, *refs):
    u_refs, gram_refs, (u_ref, row_ref) = refs[:ITERS], refs[ITERS : 2 * ITERS], refs[2 * ITERS :]
    u = y_ref[...] + scatter(recv_ref, cells_ref, y_ref.shape[1] // LANES)
    u_ref[...] = u
    columns = [(ref[0], ref[1]) for ref in gram_refs]
    columns.append(products([ref[...] for ref in u_refs] + [u], u))
    lane = lax.broadcasted_iota(jnp.int32, (8, LANES), 1)
    row = lax.broadcasted_iota(jnp.int32, (8, LANES), 0)
    placed = jnp.zeros((8, LANES), jnp.float32)
    for j in range(ITERS + 1):
        for part, total in enumerate(lane_sum(*columns[j])):
            placed = jnp.where(lane == row + (part * 64 + 8 * j), total, placed)
    row_ref[...] = jnp.broadcast_to(jnp.sum(placed, axis=0, keepdims=True), row_ref.shape)


def pair_kernel(own_ref, other_ref, msg_ref):
    total, error = two_sum(own_ref[...], other_ref[...])
    lane = lax.broadcasted_iota(jnp.int32, total.shape, 1)
    row = jnp.where(lane < 64, total, total + pltpu.roll(error, 64, 1))
    msg_ref[...] = jnp.concatenate([row] * (msg_ref.shape[0] // 8), axis=0)


def finish_kernel(count, got_ref, *refs):
    u_refs, z_refs = refs[: ITERS + 1], refs[ITERS + 1 : 2 * ITERS + 1]
    adj_ref, res_ref, flag_ref = refs[2 * ITERS + 1 :]
    lane = lax.broadcasted_iota(jnp.int32, (8, LANES), 1)
    rows = [got_ref[8 * k : 8 * k + 8, :] for k in range(count // 8)]
    pairs = [two_sum(rows[k], rows[k + 1]) for k in range(0, len(rows), 2)]
    while len(pairs) > 1:
        pairs = [dd_add(pairs[k], pairs[k + 1]) for k in range(0, len(pairs), 2)]
    total = pairs[0]
    for shift in (4, 2, 1):
        total = dd_add(total, tuple(pltpu.roll(v, shift, 0) for v in total))
    total = dd_add(total, tuple(pltpu.roll(v, 64, 1) for v in total))

    def entry(i, j):
        i, j = min(i, j), max(i, j)
        at = 8 * j + i
        return tuple(jnp.broadcast_to(v[0:1, at : at + 1], (1, LANES)) for v in total)

    n = ITERS
    mat = [[entry(i + 1, j + 1) if j >= i else None for j in range(n)] for i in range(n)]
    vec = [entry(0, i + 1) for i in range(n)]
    norms = [mat[i][i][0] for i in range(n)]
    first = entry(0, 0)
    ok = (first[0] > 1e-20) & (first[0] < 1e30)
    left = first
    scaled = [None] * n
    factor = [[None] * n for _ in range(n)]
    for k in range(n):
        pivot = mat[k][k]
        ok = ok & (norms[k] > 1e-20) & (norms[k] < 1e30) & (pivot[0] > 1e-9 * norms[k])
        inverse = 1.0 / pivot[0]
        scaled[k] = dd_over(vec[k], pivot, inverse)
        left = dd_add(left, dd_neg(dd_mul(vec[k], scaled[k])))
        for j in range(k + 1, n):
            factor[k][j] = dd_over(mat[k][j], pivot, inverse)
        for i in range(k + 1, n):
            for j in range(i, n):
                mat[i][j] = dd_add(mat[i][j], dd_neg(dd_mul(factor[k][i], mat[k][j])))
            vec[i] = dd_add(vec[i], dd_neg(dd_mul(factor[k][i], vec[k])))
    coef = [None] * n
    for k in reversed(range(n)):
        value = scaled[k]
        for j in range(k + 1, n):
            value = dd_add(value, dd_neg(dd_mul(factor[k][j], coef[j])))
        coef[k] = value
    reach = jnp.zeros((1, LANES), jnp.float32)
    for k in range(n):
        reach = reach + jnp.abs(coef[k][0]) * jnp.sqrt(norms[k])
    ok = ok & (reach * reach < 1e7 * left[0])
    flag_ref[...] = jnp.where(ok, 1, 0)
    cells = adj_ref.shape[1]
    weight = [jnp.broadcast_to(coef[k][0][:, :1], (8, cells)) for k in range(n)]
    adj = weight[0] * z_refs[0][...]
    res = u_refs[0][...] - weight[0] * u_refs[1][...]
    for k in range(1, n):
        adj = adj + weight[k] * z_refs[k][...]
        res = res - weight[k] * u_refs[k + 1][...]
    adj_ref[...] = adj[:F]
    res_ref[...] = res[:F]


def shape(*dims):
    return jax.ShapeDtypeStruct(dims, jnp.float32)


def call(kernel, out, *args, name, space=pltpu.VMEM, scratch=()):
    return pl.pallas_call(
        kernel,
        out_shape=out,
        name=name,
        in_specs=[pl.BlockSpec(memory_space=space)] * len(args),
        out_specs=tuple(
            pl.BlockSpec(memory_space=pltpu.SMEM if o.shape == (1,) else pltpu.VMEM) for o in out
        ),
        scratch_shapes=scratch,
        compiler_params=pltpu.CompilerParams(vmem_limit_bytes=24 * 2**20),
    )(*args)


def core_groups(blk, grp):
    side = math.isqrt(blk // 2)

    def distance(chip):
        place, z = chip
        return sum(min(at, size - at) for at, size in ((place // side, side), (place % side, side), (z, grp)))

    chips = sorted(((place, z) for place in range(blk // 2) for z in range(grp)), key=lambda c: (distance(c), c))
    chips = chips[-1:] + chips[:-1]
    return [[(place * 2 + core) * grp + z for place, z in chips] for core in range(2)]


def per_device(rhs, diag_blocks, lower_blocks, upper_blocks, precond, coupling, send_cells, recv_cells, halo_len):
    fields, cells = rhs.shape
    peers = send_cells.shape[1]
    count = peers * lax.axis_size("grp") // 2
    vector = shape(8, cells)
    message = shape(peers * 8, LANES)
    args = (rhs, diag_blocks, lower_blocks, upper_blocks, precond, coupling, send_cells, recv_cells, halo_len)
    blocks = (diag_blocks, lower_blocks, upper_blocks)
    gram_shape = shape(2, 8, LANES)
    inputs = (precond, coupling, send_cells, halo_len, *blocks, recv_cells)
    u, z, msg, y, gram, *kept = call(
        first_kernel,
        (vector, vector, message, vector, gram_shape, *(jax.ShapeDtypeStruct(a.shape, a.dtype) for a in inputs)),
        rhs, *inputs,
        name="first",
        space=pltpu.HBM,
        scratch=(pltpu.VMEM(rhs.shape, jnp.float32), pltpu.SemaphoreType.DMA((2 * fields + 7,))),
    )
    face, blocks, recv_cells = kept[:4], kept[4:7], kept[7]
    us, zs, grams = [u], [z], [gram]
    order = sorted(range(peers), key=lambda peer: place_of(peer, peers))
    for col in range(ITERS):
        got = lax.all_to_all(msg.reshape(peers, 8, LANES), "blk", 0, 0, axis_index_groups=[order], tiled=True)
        got = got.reshape(peers * 8, LANES)
        if col < ITERS - 1:
            u, z, msg, y, gram = call(
                functools.partial(step_kernel, col + 1),
                (vector, vector, message, vector, gram_shape),
                got, recv_cells, y, *face, *blocks, *us,
                name="step",
            )
            zs.append(z)
            grams.append(gram)
        else:
            u, row = call(last_kernel, (vector, shape(8, LANES)), got, recv_cells, y, *us, *grams, name="last")
        us.append(u)
    other = lax.ppermute(row, "blk", [(i, i ^ 1) for i in range(peers)])
    (msg,) = call(pair_kernel, (shape(count, LANES),), row, other, name="pair")
    groups = core_groups(peers, lax.axis_size("grp"))
    got = lax.all_to_all(msg, BOTH, 0, 0, axis_index_groups=groups, tiled=True)
    adjoint, residual, flag = call(
        functools.partial(finish_kernel, count),
        (shape(fields, cells), shape(fields, cells), jax.ShapeDtypeStruct((1, LANES), jnp.int32)),
        got, *us, *zs,
        name="finish",
    )
    args, adjoint, residual, flag = lax.optimization_barrier((args, adjoint, residual, flag))
    return lax.switch(flag[0, 0], [lambda *_: arnoldi(*args), lambda *outs: outs], adjoint, residual)


def solution(mesh):
    return jax.shard_map(
        per_device,
        mesh=mesh,
        in_specs=(
            P(None, BOTH),
            P(None, None, BOTH),
            P(None, None, BOTH),
            P(None, None, BOTH),
            P(None, None, BOTH),
            P(BOTH, None, None, None, None),
            P(BOTH, None, None),
            P(BOTH, None, None),
            P(BOTH, None),
        ),
        out_specs=(P(None, BOTH), P(None, BOTH)),
        check_vma=False,
    )
```

```python
import functools
import math

import jax
import jax.numpy as jnp
from jax import lax
from jax.experimental import pallas as pl
from jax.experimental.pallas import tpu as pltpu
from jax.sharding import PartitionSpec as P

ITERS = 4
F = 7
LANES = 128
BOTH = ("blk", "grp")


def mixing(blocks, field):
    total = blocks[:, 0] * field[0][None]
    for inner in range(1, field.shape[0]):
        total = total + blocks[:, inner] * field[inner][None]
    return total


def operate(field, diag_blocks, lower_blocks, upper_blocks, masked, send_flat, recv_flat):
    fields = field.shape[0]
    peers, width = masked.shape[2:]
    zero_col = jnp.zeros((fields, 1), jnp.float32)
    before = jnp.concatenate([zero_col, field[:, :-1]], axis=1)
    after = jnp.concatenate([field[:, 1:], zero_col], axis=1)
    outgoing = jnp.take(field, send_flat, axis=1).reshape(fields, peers, width)
    term = lax.all_to_all(mixing(masked, outgoing), "blk", split_axis=1, concat_axis=1, tiled=True)
    local = mixing(diag_blocks, field) + mixing(lower_blocks, before) + mixing(upper_blocks, after)
    return local.at[:, recv_flat].add(term.reshape(fields, -1))


def arnoldi(rhs, diag_blocks, lower_blocks, upper_blocks, precond, coupling, send_cells, recv_cells, halo_len):
    slots = jnp.arange(coupling.shape[4], dtype=jnp.int32)
    live = (slots[None, :] < halo_len[0][:, None]).astype(jnp.float32)
    masked = coupling[0] * live[None, None, :, :]
    send_flat = send_cells[0].reshape(-1)
    recv_flat = recv_cells[0].reshape(-1)

    def apply_op(field):
        return operate(field, diag_blocks, lower_blocks, upper_blocks, masked, send_flat, recv_flat)

    beta = jnp.sqrt(lax.psum(jnp.sum(rhs * rhs), BOTH))
    basis = [rhs / beta]
    hess = jnp.zeros((ITERS + 1, ITERS), jnp.float32)
    for col in range(ITERS):
        product = apply_op(mixing(precond, basis[col]))
        proj = lax.psum(jnp.stack([jnp.sum(vector * product) for vector in basis]), BOTH)
        remain = product
        for index in range(col + 1):
            remain = remain - proj[index] * basis[index]
        height = jnp.sqrt(lax.psum(jnp.sum(remain * remain), BOTH))
        hess = hess.at[: col + 1, col].set(proj).at[col + 1, col].set(height)
        basis.append(remain / height)
    gram = jnp.dot(hess.T, hess, precision=lax.Precision.HIGHEST)
    factor = jnp.linalg.cholesky(gram)
    coef = jax.scipy.linalg.cho_solve((factor, True), beta * hess[0])
    combo = coef[0] * basis[0]
    for index in range(1, ITERS):
        combo = combo + coef[index] * basis[index]
    adjoint = mixing(precond, combo)
    return adjoint, rhs - apply_op(adjoint)


def two_sum(a, b):
    s = a + b
    t = s - a
    return s, (a - (s - t)) + (b - t)


def quick_sum(a, b):
    s = a + b
    return s, b - (s - a)


def halves(a):
    t = a * 4097.0
    high = t - (t - a)
    return high, a - high


def two_prod(a, ah, al, b, bh, bl):
    p = a * b
    return p, ((ah * bh - p) + ah * bl + al * bh) + al * bl


def dd_add(a, b):
    s, e = two_sum(a[0], b[0])
    return quick_sum(s, e + (a[1] + b[1]))


def dd_mul(a, b):
    p, e = two_prod(a[0], *halves(a[0]), b[0], *halves(b[0]))
    return quick_sum(p, e + (a[0] * b[1] + a[1] * b[0]))


def dd_neg(a):
    return -a[0], -a[1]


def dd_over(a, b, inverse):
    q = a[0] * inverse
    rest = dd_add(a, dd_neg(dd_mul(b, (q, jnp.zeros_like(q)))))
    return quick_sum(q, rest[0] * inverse)


def turns(blk):
    side = math.isqrt(blk // 2)
    return side // 2, side // 2 * 2 + 1


def place_of(peer, blk):
    y, turn = turns(blk)
    return (y - peer // 8) % (blk // 8) * 8 + (peer - turn) % 8


def row_sums(parts):
    rows = [jnp.sum(part, axis=0, keepdims=True) for part in parts]
    return jnp.concatenate(rows + [jnp.zeros_like(rows[0])], axis=0)


def precondition(pre_ref, u):
    return row_sums([pre_ref[i] * u[:F] for i in range(F)])


def gather(z, send_ref):
    cells = z.shape[1]
    tiles = cells // LANES
    source = [
        [jnp.broadcast_to(z[f : f + 1, t * LANES : (t + 1) * LANES], (8, LANES)) for t in range(tiles)]
        for f in range(F)
    ]
    taken = []
    for q in range(send_ref.shape[1] // 8):
        cell = send_ref[0, q * 8 : (q + 1) * 8, :]
        low = cell & (LANES - 1)
        high = cell >> 7
        taken.append([])
        for f in range(F):
            got = jnp.take_along_axis(source[f][0], low, axis=1, mode="promise_in_bounds")
            for t in range(1, tiles):
                other = jnp.take_along_axis(source[f][t], low, axis=1, mode="promise_in_bounds")
                got = jnp.where(high == t, other, got)
            taken[q].append(got)
    return taken


def mix(taken, coup_ref, halo_ref, msg_ref):
    peers = halo_ref.shape[1]
    turn = turns(peers)[1]
    lanes = lax.broadcasted_iota(jnp.int32, (8, LANES), 1)
    rows = lax.broadcasted_iota(jnp.int32, (8, peers), 0)
    cols = lax.broadcasted_iota(jnp.int32, (8, peers), 1)
    lens = jnp.broadcast_to(halo_ref[...], (8, peers))
    for q in range(peers // 8):
        size = jnp.sum(jnp.where(cols == rows + q * 8, lens, 0), axis=1, keepdims=True)
        live = lanes < size
        place = place_of(q * 8, peers) // 8 * 8
        for i in range(F):
            total = coup_ref[0, i, 0, q * 8 : (q + 1) * 8, :] * taken[q][0]
            for j in range(1, F):
                total = total + coup_ref[0, i, j, q * 8 : (q + 1) * 8, :] * taken[q][j]
            msg_ref[pl.ds(place * 8 + i, 8, stride=8), :] = pltpu.roll(jnp.where(live, total, 0.0), 8 - turn, 0)
        msg_ref[pl.ds(q * 64 + F, 8, stride=8), :] = jnp.zeros((8, LANES), jnp.float32)


def scatter(recv_ref, cells_ref, tiles):
    peers = cells_ref.shape[1]
    spots = lax.broadcasted_iota(jnp.int32, (LANES, LANES), 0)
    left, right = [], []
    for s in range(peers):
        place = place_of(s, peers)
        x = recv_ref[place * 8 : (place + 1) * 8, :]
        first = x.astype(jnp.bfloat16).astype(jnp.float32)
        second = x - first
        cell = cells_ref[0, s : s + 1, :]
        low = jnp.broadcast_to(cell & (LANES - 1), (LANES, LANES))
        high = jnp.broadcast_to(cell >> 7, (8, LANES))
        pieces = []
        for t in range(tiles):
            here = high == t
            pieces += [jnp.where(here, part, 0.0) for part in (first, second)]
        left.append(jnp.concatenate(pieces, axis=0).astype(jnp.bfloat16))
        right.append(jnp.where(spots == low, 1.0, 0.0).astype(jnp.bfloat16))
    total = lax.dot_general(
        jnp.concatenate(left, axis=1),
        jnp.concatenate(right, axis=1),
        (((1,), (1,)), ((), ())),
        preferred_element_type=jnp.float32,
    )
    out = []
    for t in range(tiles):
        out.append(total[t * 16 : t * 16 + 8] + total[t * 16 + 8 : t * 16 + 16])
    return jnp.concatenate(out, axis=1)


def local_part(z, diag_ref, low_ref, up_ref):
    cells = z.shape[1]
    col = lax.broadcasted_iota(jnp.int32, z.shape, 1)
    before = jnp.where(col == 0, 0.0, pltpu.roll(z, 1, 1))[:F]
    after = jnp.where(col == cells - 1, 0.0, pltpu.roll(z, cells - 1, 1))[:F]
    z = z[:F]
    return row_sums([diag_ref[i] * z + low_ref[i] * before + up_ref[i] * after for i in range(F)])


def products(us, last):
    cells = last.shape[1]
    tiles = [slice(t * LANES, (t + 1) * LANES) for t in range(cells // LANES)]
    lh, ll = halves(last)
    rows = lax.broadcasted_iota(jnp.int32, (8, LANES), 0)
    hi = jnp.zeros((8, LANES), jnp.float32)
    lo = jnp.zeros((8, LANES), jnp.float32)
    for i, u in enumerate(us):
        uh, ul = halves(u)
        terms = []
        for t in tiles:
            terms.append(two_prod(u[:, t], uh[:, t], ul[:, t], last[:, t], lh[:, t], ll[:, t]))
        while len(terms) > 1:
            terms = [dd_add(terms[k], terms[k + 1]) for k in range(0, len(terms), 2)]
        total = terms[0]
        for shift in (4, 2, 1):
            total = dd_add(total, tuple(pltpu.roll(v, shift, 0) for v in total))
        hi = jnp.where(rows == i, total[0], hi)
        lo = jnp.where(rows == i, total[1], lo)
    return hi, lo


def lane_sum(hi, lo):
    top = jnp.max(jnp.abs(hi), axis=1, keepdims=True) * 8192.0
    coarse = (hi + top) - top
    fine = (hi - coarse) + lo
    return quick_sum(jnp.sum(coarse, axis=1, keepdims=True), jnp.sum(fine, axis=1, keepdims=True))


def first_kernel(
    rhs_hbm, pre_hbm, coup_hbm, send_hbm, halo_hbm, diag_hbm, low_hbm, up_hbm, cells_hbm,
    u_ref, z_ref, msg_ref, y_ref, gram_ref, pre_ref, coup_ref, send_ref, halo_ref, diag_ref, low_ref, up_ref, cells_ref,
    rhs_ref, sems,
):
    whole = [(rhs_hbm, rhs_ref), (send_hbm, send_ref), (halo_hbm, halo_ref)]
    rows = [(pre_hbm, pre_ref)]
    faces = [(coup_hbm, coup_ref)]
    blocks = [(diag_hbm, diag_ref), (low_hbm, low_ref), (up_hbm, up_ref), (cells_hbm, cells_ref)]
    copies = [pltpu.make_async_copy(*pair, sems.at[k]) for k, pair in enumerate(whole + rows + faces + blocks)]
    for copy in copies:
        copy.start()
    for copy in copies[: len(whole)]:
        copy.wait()
    u = jnp.concatenate([rhs_ref[...], jnp.zeros((1, rhs_ref.shape[1]), jnp.float32)], axis=0)
    u_ref[...] = u
    gram_ref[0], gram_ref[1] = products([u], u)
    for copy in copies[len(whole) : len(whole) + 1]:
        copy.wait()
    z = precondition(pre_ref, u)
    z_ref[...] = z
    taken = gather(z, send_ref)
    for copy in copies[len(whole) + 1 : len(whole) + 2]:
        copy.wait()
    mix(taken, coup_ref, halo_ref, msg_ref)
    for copy in copies[len(whole) + 2 :]:
        copy.wait()
    y_ref[...] = local_part(z, diag_ref, low_ref, up_ref)


def step_kernel(col, recv_ref, cells_ref, y_ref, pre_ref, coup_ref, send_ref, halo_ref, diag_ref, low_ref, up_ref, *refs):
    u_refs, (u_ref, z_ref, msg_ref, next_ref, gram_ref) = refs[:col], refs[col:]
    u = y_ref[...] + scatter(recv_ref, cells_ref, y_ref.shape[1] // LANES)
    z = precondition(pre_ref, u)
    u_ref[...] = u
    z_ref[...] = z
    mix(gather(z, send_ref), coup_ref, halo_ref, msg_ref)
    next_ref[...] = local_part(z, diag_ref, low_ref, up_ref)
    gram_ref[0], gram_ref[1] = products([ref[...] for ref in u_refs] + [u], u)


def last_kernel(recv_ref, cells_ref, y_ref, *refs):
    u_refs, gram_refs, (u_ref, row_ref) = refs[:ITERS], refs[ITERS : 2 * ITERS], refs[2 * ITERS :]
    u = y_ref[...] + scatter(recv_ref, cells_ref, y_ref.shape[1] // LANES)
    u_ref[...] = u
    columns = [(ref[0], ref[1]) for ref in gram_refs]
    columns.append(products([ref[...] for ref in u_refs] + [u], u))
    lane = lax.broadcasted_iota(jnp.int32, (8, LANES), 1)
    row = lax.broadcasted_iota(jnp.int32, (8, LANES), 0)
    placed = jnp.zeros((8, LANES), jnp.float32)
    for j in range(ITERS + 1):
        for part, total in enumerate(lane_sum(*columns[j])):
            placed = jnp.where(lane == row + (part * 64 + 8 * j), total, placed)
    row_ref[...] = jnp.broadcast_to(jnp.sum(placed, axis=0, keepdims=True), row_ref.shape)


def pair_kernel(own_ref, other_ref, msg_ref):
    own, other = own_ref[...], other_ref[...]
    ahead = jnp.abs(own) >= jnp.abs(other)
    total, error = quick_sum(jnp.where(ahead, own, other), jnp.where(ahead, other, own))
    lane = lax.broadcasted_iota(jnp.int32, total.shape, 1)
    row = jnp.where(lane < 64, total, total + pltpu.roll(error, 64, 1))
    msg_ref[...] = jnp.concatenate([row] * (msg_ref.shape[0] // 8), axis=0)


def finish_kernel(count, got_ref, *refs):
    u_refs, z_refs = refs[: ITERS + 1], refs[ITERS + 1 : 2 * ITERS + 1]
    adj_ref, res_ref, flag_ref = refs[2 * ITERS + 1 :]
    lane = lax.broadcasted_iota(jnp.int32, (8, LANES), 1)
    rows = [got_ref[8 * k : 8 * k + 8, :] for k in range(count // 8)]
    pairs = [two_sum(rows[k], rows[k + 1]) for k in range(0, len(rows), 2)]
    while len(pairs) > 1:
        pairs = [dd_add(pairs[k], pairs[k + 1]) for k in range(0, len(pairs), 2)]
    total = pairs[0]
    for shift in (4, 2, 1):
        total = dd_add(total, tuple(pltpu.roll(v, shift, 0) for v in total))
    total = dd_add(total, tuple(pltpu.roll(v, 64, 1) for v in total))

    def entry(i, j):
        i, j = min(i, j), max(i, j)
        at = 8 * j + i
        return tuple(jnp.broadcast_to(v[0:1, at : at + 1], (1, LANES)) for v in total)

    n = ITERS
    mat = [[entry(i + 1, j + 1) if j >= i else None for j in range(n)] for i in range(n)]
    vec = [entry(0, i + 1) for i in range(n)]
    norms = [mat[i][i][0] for i in range(n)]
    first = entry(0, 0)
    ok = (first[0] > 1e-20) & (first[0] < 1e30)
    left = first
    scaled = [None] * n
    factor = [[None] * n for _ in range(n)]
    for k in range(n):
        pivot = mat[k][k]
        ok = ok & (norms[k] > 1e-20) & (norms[k] < 1e30) & (pivot[0] > 1e-9 * norms[k])
        inverse = 1.0 / pivot[0]
        scaled[k] = dd_over(vec[k], pivot, inverse)
        left = dd_add(left, dd_neg(dd_mul(vec[k], scaled[k])))
        for j in range(k + 1, n):
            factor[k][j] = dd_over(mat[k][j], pivot, inverse)
        for i in range(k + 1, n):
            for j in range(i, n):
                mat[i][j] = dd_add(mat[i][j], dd_neg(dd_mul(factor[k][i], mat[k][j])))
            vec[i] = dd_add(vec[i], dd_neg(dd_mul(factor[k][i], vec[k])))
    coef = [None] * n
    for k in reversed(range(n)):
        value = scaled[k]
        for j in range(k + 1, n):
            value = dd_add(value, dd_neg(dd_mul(factor[k][j], coef[j])))
        coef[k] = value
    reach = jnp.zeros((1, LANES), jnp.float32)
    for k in range(n):
        reach = reach + jnp.abs(coef[k][0]) * jnp.sqrt(norms[k])
    ok = ok & (reach * reach < 1e7 * left[0])
    flag_ref[...] = jnp.where(ok, 1, 0)
    cells = adj_ref.shape[1]
    weight = [jnp.broadcast_to(coef[k][0][:, :1], (8, cells)) for k in range(n)]
    adj = weight[0] * z_refs[0][...]
    res = u_refs[0][...] - weight[0] * u_refs[1][...]
    for k in range(1, n):
        adj = adj + weight[k] * z_refs[k][...]
        res = res - weight[k] * u_refs[k + 1][...]
    adj_ref[...] = adj[:F]
    res_ref[...] = res[:F]


def shape(*dims):
    return jax.ShapeDtypeStruct(dims, jnp.float32)


def call(kernel, out, *args, name, space=pltpu.VMEM, scratch=()):
    return pl.pallas_call(
        kernel,
        out_shape=out,
        name=name,
        in_specs=[pl.BlockSpec(memory_space=space)] * len(args),
        out_specs=tuple(
            pl.BlockSpec(memory_space=pltpu.SMEM if o.shape == (1,) else pltpu.VMEM) for o in out
        ),
        scratch_shapes=scratch,
        compiler_params=pltpu.CompilerParams(vmem_limit_bytes=24 * 2**20),
    )(*args)


def core_groups(blk, grp):
    side = math.isqrt(blk // 2)

    def distance(chip):
        place, z = chip
        return sum(min(at, size - at) for at, size in ((place // side, side), (place % side, side), (z, grp)))

    chips = sorted(((place, z) for place in range(blk // 2) for z in range(grp)), key=lambda c: (distance(c), c))
    chips = chips[-1:] + chips[:-1]
    return [[(place * 2 + core) * grp + z for place, z in chips] for core in range(2)]


def per_device(rhs, diag_blocks, lower_blocks, upper_blocks, precond, coupling, send_cells, recv_cells, halo_len):
    fields, cells = rhs.shape
    peers = send_cells.shape[1]
    count = peers * lax.axis_size("grp") // 2
    vector = shape(8, cells)
    message = shape(peers * 8, LANES)
    args = (rhs, diag_blocks, lower_blocks, upper_blocks, precond, coupling, send_cells, recv_cells, halo_len)
    blocks = (diag_blocks, lower_blocks, upper_blocks)
    gram_shape = shape(2, 8, LANES)
    inputs = (precond, coupling, send_cells, halo_len, *blocks, recv_cells)
    u, z, msg, y, gram, *kept = call(
        first_kernel,
        (vector, vector, message, vector, gram_shape, *(jax.ShapeDtypeStruct(a.shape, a.dtype) for a in inputs)),
        rhs, *inputs,
        name="first",
        space=pltpu.HBM,
        scratch=(pltpu.VMEM(rhs.shape, jnp.float32), pltpu.SemaphoreType.DMA((2 * fields + 7,))),
    )
    face, blocks, recv_cells = kept[:4], kept[4:7], kept[7]
    us, zs, grams = [u], [z], [gram]
    order = sorted(range(peers), key=lambda peer: place_of(peer, peers))
    for col in range(ITERS):
        got = lax.all_to_all(msg.reshape(peers, 8, LANES), "blk", 0, 0, axis_index_groups=[order], tiled=True)
        got = got.reshape(peers * 8, LANES)
        if col < ITERS - 1:
            u, z, msg, y, gram = call(
                functools.partial(step_kernel, col + 1),
                (vector, vector, message, vector, gram_shape),
                got, recv_cells, y, *face, *blocks, *us,
                name="step",
            )
            zs.append(z)
            grams.append(gram)
        else:
            u, row = call(last_kernel, (vector, shape(8, LANES)), got, recv_cells, y, *us, *grams, name="last")
        us.append(u)
    other = lax.ppermute(row, "blk", [(i, i ^ 1) for i in range(peers)])
    (msg,) = call(pair_kernel, (shape(count, LANES),), row, other, name="pair")
    groups = core_groups(peers, lax.axis_size("grp"))
    got = lax.all_to_all(msg, BOTH, 0, 0, axis_index_groups=groups, tiled=True)
    adjoint, residual, flag = call(
        functools.partial(finish_kernel, count),
        (shape(fields, cells), shape(fields, cells), jax.ShapeDtypeStruct((1, LANES), jnp.int32)),
        got, *us, *zs,
        name="finish",
    )
    args, adjoint, residual, flag = lax.optimization_barrier((args, adjoint, residual, flag))
    return lax.switch(flag[0, 0], [lambda *_: arnoldi(*args), lambda *outs: outs], adjoint, residual)


def solution(mesh):
    return jax.shard_map(
        per_device,
        mesh=mesh,
        in_specs=(
            P(None, BOTH),
            P(None, None, BOTH),
            P(None, None, BOTH),
            P(None, None, BOTH),
            P(None, None, BOTH),
            P(BOTH, None, None, None, None),
            P(BOTH, None, None),
            P(BOTH, None, None),
            P(BOTH, None),
        ),
        out_specs=(P(None, BOTH), P(None, BOTH)),
        check_vma=False,
    )
```

```python
import functools
import math

import jax
import jax.numpy as jnp
from jax import lax
from jax.experimental import pallas as pl
from jax.experimental.pallas import tpu as pltpu
from jax.sharding import PartitionSpec as P

ITERS = 4
F = 7
LANES = 128
BOTH = ("blk", "grp")


def mixing(blocks, field):
    total = blocks[:, 0] * field[0][None]
    for inner in range(1, field.shape[0]):
        total = total + blocks[:, inner] * field[inner][None]
    return total


def operate(field, diag_blocks, lower_blocks, upper_blocks, masked, send_flat, recv_flat):
    fields = field.shape[0]
    peers, width = masked.shape[2:]
    zero_col = jnp.zeros((fields, 1), jnp.float32)
    before = jnp.concatenate([zero_col, field[:, :-1]], axis=1)
    after = jnp.concatenate([field[:, 1:], zero_col], axis=1)
    outgoing = jnp.take(field, send_flat, axis=1).reshape(fields, peers, width)
    term = lax.all_to_all(mixing(masked, outgoing), "blk", split_axis=1, concat_axis=1, tiled=True)
    local = mixing(diag_blocks, field) + mixing(lower_blocks, before) + mixing(upper_blocks, after)
    return local.at[:, recv_flat].add(term.reshape(fields, -1))


def arnoldi(rhs, diag_blocks, lower_blocks, upper_blocks, precond, coupling, send_cells, recv_cells, halo_len):
    slots = jnp.arange(coupling.shape[4], dtype=jnp.int32)
    live = (slots[None, :] < halo_len[0][:, None]).astype(jnp.float32)
    masked = coupling[0] * live[None, None, :, :]
    send_flat = send_cells[0].reshape(-1)
    recv_flat = recv_cells[0].reshape(-1)

    def apply_op(field):
        return operate(field, diag_blocks, lower_blocks, upper_blocks, masked, send_flat, recv_flat)

    beta = jnp.sqrt(lax.psum(jnp.sum(rhs * rhs), BOTH))
    basis = [rhs / beta]
    hess = jnp.zeros((ITERS + 1, ITERS), jnp.float32)
    for col in range(ITERS):
        product = apply_op(mixing(precond, basis[col]))
        proj = lax.psum(jnp.stack([jnp.sum(vector * product) for vector in basis]), BOTH)
        remain = product
        for index in range(col + 1):
            remain = remain - proj[index] * basis[index]
        height = jnp.sqrt(lax.psum(jnp.sum(remain * remain), BOTH))
        hess = hess.at[: col + 1, col].set(proj).at[col + 1, col].set(height)
        basis.append(remain / height)
    gram = jnp.dot(hess.T, hess, precision=lax.Precision.HIGHEST)
    factor = jnp.linalg.cholesky(gram)
    coef = jax.scipy.linalg.cho_solve((factor, True), beta * hess[0])
    combo = coef[0] * basis[0]
    for index in range(1, ITERS):
        combo = combo + coef[index] * basis[index]
    adjoint = mixing(precond, combo)
    return adjoint, rhs - apply_op(adjoint)


def two_sum(a, b):
    s = a + b
    t = s - a
    return s, (a - (s - t)) + (b - t)


def quick_sum(a, b):
    s = a + b
    return s, b - (s - a)


def halves(a):
    t = a * 4097.0
    high = t - (t - a)
    return high, a - high


def two_prod(a, ah, al, b, bh, bl):
    p = a * b
    return p, ((ah * bh - p) + ah * bl + al * bh) + al * bl


def dd_add(a, b):
    s, e = two_sum(a[0], b[0])
    return quick_sum(s, e + (a[1] + b[1]))


def dd_mul(a, b):
    p, e = two_prod(a[0], *halves(a[0]), b[0], *halves(b[0]))
    return quick_sum(p, e + (a[0] * b[1] + a[1] * b[0]))


def dd_neg(a):
    return -a[0], -a[1]


def dd_over(a, b, inverse):
    q = a[0] * inverse
    rest = dd_add(a, dd_neg(dd_mul(b, (q, jnp.zeros_like(q)))))
    return quick_sum(q, rest[0] * inverse)


def turns(blk):
    side = math.isqrt(blk // 2)
    return side // 2, side // 2 * 2 + 1


def place_of(peer, blk):
    y, turn = turns(blk)
    return (y - peer // 8) % (blk // 8) * 8 + (peer - turn) % 8


def row_sums(parts):
    rows = [jnp.sum(part, axis=0, keepdims=True) for part in parts]
    return jnp.concatenate(rows + [jnp.zeros_like(rows[0])], axis=0)


def precondition(pre_ref, u):
    return row_sums([pre_ref[i] * u[:F] for i in range(F)])


def gather(z, send_ref):
    cells = z.shape[1]
    tiles = cells // LANES
    source = [
        [jnp.broadcast_to(z[f : f + 1, t * LANES : (t + 1) * LANES], (8, LANES)) for t in range(tiles)]
        for f in range(F)
    ]
    taken = []
    for q in range(send_ref.shape[1] // 8):
        cell = send_ref[0, q * 8 : (q + 1) * 8, :]
        low = cell & (LANES - 1)
        high = cell >> 7
        taken.append([])
        for f in range(F):
            got = jnp.take_along_axis(source[f][0], low, axis=1, mode="promise_in_bounds")
            for t in range(1, tiles):
                other = jnp.take_along_axis(source[f][t], low, axis=1, mode="promise_in_bounds")
                got = jnp.where(high == t, other, got)
            taken[q].append(got)
    return taken


def mix(taken, coup_ref, halo_ref, msg_ref):
    peers = halo_ref.shape[1]
    turn = turns(peers)[1]
    lanes = lax.broadcasted_iota(jnp.int32, (8, LANES), 1)
    rows = lax.broadcasted_iota(jnp.int32, (8, peers), 0)
    cols = lax.broadcasted_iota(jnp.int32, (8, peers), 1)
    lens = jnp.broadcast_to(halo_ref[...], (8, peers))
    for q in range(peers // 8):
        size = jnp.sum(jnp.where(cols == rows + q * 8, lens, 0), axis=1, keepdims=True)
        live = lanes < size
        place = place_of(q * 8, peers) // 8 * 8
        for i in range(F):
            total = coup_ref[0, i, 0, q * 8 : (q + 1) * 8, :] * taken[q][0]
            for j in range(1, F):
                total = total + coup_ref[0, i, j, q * 8 : (q + 1) * 8, :] * taken[q][j]
            msg_ref[pl.ds(place * 8 + i, 8, stride=8), :] = pltpu.roll(jnp.where(live, total, 0.0), 8 - turn, 0)
        msg_ref[pl.ds(q * 64 + F, 8, stride=8), :] = jnp.zeros((8, LANES), jnp.float32)


def scatter(recv_ref, cells_ref, tiles):
    peers = cells_ref.shape[1]
    spots = lax.broadcasted_iota(jnp.int32, (LANES, LANES), 0)
    left, right = [], []
    for s in range(peers):
        place = place_of(s, peers)
        x = recv_ref[place * 8 : (place + 1) * 8, :]
        first = x.astype(jnp.bfloat16).astype(jnp.float32)
        second = x - first
        cell = cells_ref[0, s : s + 1, :]
        low = jnp.broadcast_to(cell & (LANES - 1), (LANES, LANES))
        high = jnp.broadcast_to(cell >> 7, (8, LANES))
        pieces = []
        for t in range(tiles):
            here = high == t
            pieces += [jnp.where(here, part, 0.0) for part in (first, second)]
        left.append(jnp.concatenate(pieces, axis=0).astype(jnp.bfloat16))
        right.append(jnp.where(spots == low, 1.0, 0.0).astype(jnp.bfloat16))
    total = lax.dot_general(
        jnp.concatenate(left, axis=1),
        jnp.concatenate(right, axis=1),
        (((1,), (1,)), ((), ())),
        preferred_element_type=jnp.float32,
    )
    out = []
    for t in range(tiles):
        out.append(total[t * 16 : t * 16 + 8] + total[t * 16 + 8 : t * 16 + 16])
    return jnp.concatenate(out, axis=1)


def local_part(z, diag_ref, low_ref, up_ref):
    cells = z.shape[1]
    col = lax.broadcasted_iota(jnp.int32, z.shape, 1)
    before = jnp.where(col == 0, 0.0, pltpu.roll(z, 1, 1))[:F]
    after = jnp.where(col == cells - 1, 0.0, pltpu.roll(z, cells - 1, 1))[:F]
    z = z[:F]
    return row_sums([diag_ref[i] * z + low_ref[i] * before + up_ref[i] * after for i in range(F)])


def products(us, last):
    cells = last.shape[1]
    tiles = [slice(t * LANES, (t + 1) * LANES) for t in range(cells // LANES)]
    lh, ll = halves(last)
    rows = lax.broadcasted_iota(jnp.int32, (8, LANES), 0)
    hi = jnp.zeros((8, LANES), jnp.float32)
    lo = jnp.zeros((8, LANES), jnp.float32)
    for i, u in enumerate(us):
        uh, ul = halves(u)
        terms = []
        for t in tiles:
            terms.append(two_prod(u[:, t], uh[:, t], ul[:, t], last[:, t], lh[:, t], ll[:, t]))
        while len(terms) > 1:
            terms = [dd_add(terms[k], terms[k + 1]) for k in range(0, len(terms), 2)]
        total = terms[0]
        for shift in (4, 2, 1):
            total = dd_add(total, tuple(pltpu.roll(v, shift, 0) for v in total))
        hi = jnp.where(rows == i, total[0], hi)
        lo = jnp.where(rows == i, total[1], lo)
    return hi, lo


def lane_sum(hi, lo):
    top = jnp.max(jnp.abs(hi), axis=1, keepdims=True) * 8192.0
    coarse = (hi + top) - top
    fine = (hi - coarse) + lo
    return quick_sum(jnp.sum(coarse, axis=1, keepdims=True), jnp.sum(fine, axis=1, keepdims=True))


def first_kernel(
    rhs_hbm, pre_hbm, coup_hbm, send_hbm, halo_hbm, diag_hbm, low_hbm, up_hbm, cells_hbm,
    u_ref, z_ref, msg_ref, y_ref, gram_ref, pre_ref, coup_ref, send_ref, halo_ref, diag_ref, low_ref, up_ref, cells_ref,
    rhs_ref, sems,
):
    whole = [(rhs_hbm, rhs_ref), (send_hbm, send_ref), (halo_hbm, halo_ref)]
    rows = [(pre_hbm, pre_ref)]
    faces = [(coup_hbm, coup_ref)]
    blocks = [(diag_hbm, diag_ref), (low_hbm, low_ref), (up_hbm, up_ref), (cells_hbm, cells_ref)]
    copies = [pltpu.make_async_copy(*pair, sems.at[k]) for k, pair in enumerate(whole + rows + blocks + faces)]
    for copy in copies:
        copy.start()
    for copy in copies[: len(whole)]:
        copy.wait()
    u = jnp.concatenate([rhs_ref[...], jnp.zeros((1, rhs_ref.shape[1]), jnp.float32)], axis=0)
    u_ref[...] = u
    gram_ref[0], gram_ref[1] = products([u], u)
    for copy in copies[len(whole) : len(whole) + 1]:
        copy.wait()
    z = precondition(pre_ref, u)
    z_ref[...] = z
    taken = gather(z, send_ref)
    for copy in copies[len(whole) + 1 : -1]:
        copy.wait()
    y_ref[...] = local_part(z, diag_ref, low_ref, up_ref)
    copies[-1].wait()
    mix(taken, coup_ref, halo_ref, msg_ref)


def step_kernel(col, recv_ref, cells_ref, y_ref, pre_ref, coup_ref, send_ref, halo_ref, diag_ref, low_ref, up_ref, *refs):
    u_refs, (u_ref, z_ref, msg_ref, next_ref, gram_ref) = refs[:col], refs[col:]
    u = y_ref[...] + scatter(recv_ref, cells_ref, y_ref.shape[1] // LANES)
    z = precondition(pre_ref, u)
    u_ref[...] = u
    z_ref[...] = z
    mix(gather(z, send_ref), coup_ref, halo_ref, msg_ref)
    next_ref[...] = local_part(z, diag_ref, low_ref, up_ref)
    gram_ref[0], gram_ref[1] = products([ref[...] for ref in u_refs] + [u], u)


def last_kernel(recv_ref, cells_ref, y_ref, *refs):
    u_refs, gram_refs, (u_ref, row_ref) = refs[:ITERS], refs[ITERS : 2 * ITERS], refs[2 * ITERS :]
    u = y_ref[...] + scatter(recv_ref, cells_ref, y_ref.shape[1] // LANES)
    u_ref[...] = u
    columns = [(ref[0], ref[1]) for ref in gram_refs]
    columns.append(products([ref[...] for ref in u_refs] + [u], u))
    lane = lax.broadcasted_iota(jnp.int32, (8, LANES), 1)
    row = lax.broadcasted_iota(jnp.int32, (8, LANES), 0)
    placed = jnp.zeros((8, LANES), jnp.float32)
    for j in range(ITERS + 1):
        for part, total in enumerate(lane_sum(*columns[j])):
            placed = jnp.where(lane == row + (part * 64 + 8 * j), total, placed)
    row_ref[...] = jnp.broadcast_to(jnp.sum(placed, axis=0, keepdims=True), row_ref.shape)


def pair_kernel(own_ref, other_ref, msg_ref):
    own, other = own_ref[...], other_ref[...]
    ahead = jnp.abs(own) >= jnp.abs(other)
    total, error = quick_sum(jnp.where(ahead, own, other), jnp.where(ahead, other, own))
    lane = lax.broadcasted_iota(jnp.int32, total.shape, 1)
    row = jnp.where(lane < 64, total, total + pltpu.roll(error, 64, 1))
    msg_ref[...] = jnp.concatenate([row] * (msg_ref.shape[0] // 8), axis=0)


def finish_kernel(count, got_ref, *refs):
    u_refs, z_refs = refs[: ITERS + 1], refs[ITERS + 1 : 2 * ITERS + 1]
    adj_ref, res_ref, flag_ref = refs[2 * ITERS + 1 :]
    lane = lax.broadcasted_iota(jnp.int32, (8, LANES), 1)
    rows = [got_ref[8 * k : 8 * k + 8, :] for k in range(count // 8)]
    pairs = [two_sum(rows[k], rows[k + 1]) for k in range(0, len(rows), 2)]
    while len(pairs) > 1:
        pairs = [dd_add(pairs[k], pairs[k + 1]) for k in range(0, len(pairs), 2)]
    total = pairs[0]
    for shift in (4, 2, 1):
        total = dd_add(total, tuple(pltpu.roll(v, shift, 0) for v in total))
    total = dd_add(total, tuple(pltpu.roll(v, 64, 1) for v in total))

    def entry(i, j):
        i, j = min(i, j), max(i, j)
        at = 8 * j + i
        return tuple(jnp.broadcast_to(v[0:1, at : at + 1], (1, LANES)) for v in total)

    n = ITERS
    mat = [[entry(i + 1, j + 1) if j >= i else None for j in range(n)] for i in range(n)]
    vec = [entry(0, i + 1) for i in range(n)]
    norms = [mat[i][i][0] for i in range(n)]
    first = entry(0, 0)
    ok = (first[0] > 1e-20) & (first[0] < 1e30)
    left = first
    scaled = [None] * n
    factor = [[None] * n for _ in range(n)]
    for k in range(n):
        pivot = mat[k][k]
        ok = ok & (norms[k] > 1e-20) & (norms[k] < 1e30) & (pivot[0] > 1e-9 * norms[k])
        inverse = 1.0 / pivot[0]
        scaled[k] = dd_over(vec[k], pivot, inverse)
        left = dd_add(left, dd_neg(dd_mul(vec[k], scaled[k])))
        for j in range(k + 1, n):
            factor[k][j] = dd_over(mat[k][j], pivot, inverse)
        for i in range(k + 1, n):
            for j in range(i, n):
                mat[i][j] = dd_add(mat[i][j], dd_neg(dd_mul(factor[k][i], mat[k][j])))
            vec[i] = dd_add(vec[i], dd_neg(dd_mul(factor[k][i], vec[k])))
    coef = [None] * n
    for k in reversed(range(n)):
        value = scaled[k]
        for j in range(k + 1, n):
            value = dd_add(value, dd_neg(dd_mul(factor[k][j], coef[j])))
        coef[k] = value
    reach = jnp.zeros((1, LANES), jnp.float32)
    for k in range(n):
        reach = reach + jnp.abs(coef[k][0]) * jnp.sqrt(norms[k])
    ok = ok & (reach * reach < 1e7 * left[0])
    flag_ref[...] = jnp.where(ok, 1, 0)
    cells = adj_ref.shape[1]
    weight = [jnp.broadcast_to(coef[k][0][:, :1], (8, cells)) for k in range(n)]
    adj = weight[0] * z_refs[0][...]
    res = u_refs[0][...] - weight[0] * u_refs[1][...]
    for k in range(1, n):
        adj = adj + weight[k] * z_refs[k][...]
        res = res - weight[k] * u_refs[k + 1][...]
    adj_ref[...] = adj[:F]
    res_ref[...] = res[:F]


def shape(*dims):
    return jax.ShapeDtypeStruct(dims, jnp.float32)


def call(kernel, out, *args, name, space=pltpu.VMEM, scratch=()):
    return pl.pallas_call(
        kernel,
        out_shape=out,
        name=name,
        in_specs=[pl.BlockSpec(memory_space=space)] * len(args),
        out_specs=tuple(
            pl.BlockSpec(memory_space=pltpu.SMEM if o.shape == (1,) else pltpu.VMEM) for o in out
        ),
        scratch_shapes=scratch,
        compiler_params=pltpu.CompilerParams(vmem_limit_bytes=24 * 2**20),
    )(*args)


def core_groups(blk, grp):
    side = math.isqrt(blk // 2)

    def distance(chip):
        place, z = chip
        return sum(min(at, size - at) for at, size in ((place // side, side), (place % side, side), (z, grp)))

    chips = sorted(((place, z) for place in range(blk // 2) for z in range(grp)), key=lambda c: (distance(c), c))
    chips = chips[-1:] + chips[:-1]
    return [[(place * 2 + core) * grp + z for place, z in chips] for core in range(2)]


def per_device(rhs, diag_blocks, lower_blocks, upper_blocks, precond, coupling, send_cells, recv_cells, halo_len):
    fields, cells = rhs.shape
    peers = send_cells.shape[1]
    count = peers * lax.axis_size("grp") // 2
    vector = shape(8, cells)
    message = shape(peers * 8, LANES)
    args = (rhs, diag_blocks, lower_blocks, upper_blocks, precond, coupling, send_cells, recv_cells, halo_len)
    blocks = (diag_blocks, lower_blocks, upper_blocks)
    gram_shape = shape(2, 8, LANES)
    inputs = (precond, coupling, send_cells, halo_len, *blocks, recv_cells)
    u, z, msg, y, gram, *kept = call(
        first_kernel,
        (vector, vector, message, vector, gram_shape, *(jax.ShapeDtypeStruct(a.shape, a.dtype) for a in inputs)),
        rhs, *inputs,
        name="first",
        space=pltpu.HBM,
        scratch=(pltpu.VMEM(rhs.shape, jnp.float32), pltpu.SemaphoreType.DMA((2 * fields + 7,))),
    )
    face, blocks, recv_cells = kept[:4], kept[4:7], kept[7]
    us, zs, grams = [u], [z], [gram]
    order = sorted(range(peers), key=lambda peer: place_of(peer, peers))
    for col in range(ITERS):
        got = lax.all_to_all(msg.reshape(peers, 8, LANES), "blk", 0, 0, axis_index_groups=[order], tiled=True)
        got = got.reshape(peers * 8, LANES)
        if col < ITERS - 1:
            u, z, msg, y, gram = call(
                functools.partial(step_kernel, col + 1),
                (vector, vector, message, vector, gram_shape),
                got, recv_cells, y, *face, *blocks, *us,
                name="step",
            )
            zs.append(z)
            grams.append(gram)
        else:
            u, row = call(last_kernel, (vector, shape(8, LANES)), got, recv_cells, y, *us, *grams, name="last")
        us.append(u)
    other = lax.ppermute(row, "blk", [(i, i ^ 1) for i in range(peers)])
    (msg,) = call(pair_kernel, (shape(count, LANES),), row, other, name="pair")
    groups = core_groups(peers, lax.axis_size("grp"))
    got = lax.all_to_all(msg, BOTH, 0, 0, axis_index_groups=groups, tiled=True)
    adjoint, residual, flag = call(
        functools.partial(finish_kernel, count),
        (shape(fields, cells), shape(fields, cells), jax.ShapeDtypeStruct((1, LANES), jnp.int32)),
        got, *us, *zs,
        name="finish",
    )
    args, adjoint, residual, flag = lax.optimization_barrier((args, adjoint, residual, flag))
    return lax.switch(flag[0, 0], [lambda *_: arnoldi(*args), lambda *outs: outs], adjoint, residual)


def solution(mesh):
    return jax.shard_map(
        per_device,
        mesh=mesh,
        in_specs=(
            P(None, BOTH),
            P(None, None, BOTH),
            P(None, None, BOTH),
            P(None, None, BOTH),
            P(None, None, BOTH),
            P(BOTH, None, None, None, None),
            P(BOTH, None, None),
            P(BOTH, None, None),
            P(BOTH, None),
        ),
        out_specs=(P(None, BOTH), P(None, BOTH)),
        check_vma=False,
    )
```
